128 devices in a mesh: blk: 64 (over x, z, y), rep: 2 (over core).
Axes of the slice: x: 4, y: 4, z: 4, core: 2. Of those that a mesh axis runs over, the one named last changes fastest.
Arguments:
- sky_map: float32 [2048, 32768], P('blk', 'rep'), may hold values from -6 to 6
- noise_weight: float32 [2048, 32768], P('blk', 'rep'), may hold values from 0.25 to 4
- prior_weight: float32 [512, 4, 2, 128], P('blk', 'rep'), may hold values from 0.5 to 4
- seeds: float32 [512, 4, 2, 2048], P('blk', 'rep'), may hold values from -5 to 5
- loop_cos: float32 [2048], replicated, may hold values from -0.3 to 0.3
- pair_m: int32 [512, 2], replicated, may hold values from 1 to 14939
- block_count: int32 [512], P('blk'), may hold values from 1 to 3, as said below
Outputs:
- solution: float32 [512, 4, 2, 128], P('blk', 'rep')
- residual: float32 [512, 4, 2, 128], P('blk', 'rep')
The draws below stay inside these ranges and needn't reach their ends.
Inputs may be any that keep to these rules, and one draw needn't show every extreme that they name: `pair_m`: each pair holds two m-columns; values may repeat between pairs. Pair p's first block_count[p] l-blocks belong to its first column, the other 4 - block_count[p] to its second.
All inputs are finite; a program needn't handle non-finite values.
Results may differ from the reference program's by a relative error of at most 0.00045.
Values sent between devices are 32-bit elements; how exact they have to be, the bound alone decides.
No kernel may reach another device: no remote copies, remote signals or barrier semaphores. Data moves between devices by JAX's collectives and lax.ppermute only.
A program may use at most 128 MiB of HBM per device.

```python
import math
import jax
import jax.numpy as jnp
from jax import lax

NPHI = 32768
NBP = 4
ITERS = 2
NRING = 2048
NPAIRS = 512
NCOL = 1024
MMAX = 14939


def draw_block_count(key, part):
    counts = 1 + jnp.arange(NPAIRS, dtype=jnp.int32) % (NBP - 1)
    return jax.random.permutation(key, counts).astype(jnp.int32)


def set_ends(values, own_key, low, high):
    place = [jax.random.randint(jax.random.fold_in(own_key, axis), (), 0, length) for axis, length in enumerate(values.shape)]
    longest = values.shape.index(max(values.shape))
    next_to = place[:longest] + [(place[longest] + 1) % values.shape[longest]] + place[longest + 1:]
    return values.at[tuple(place)].set(low).at[tuple(next_to)].set(high)


def levels(own_key, extent, shards, low, high):
    level, own = 1.0, jax.random.fold_in(own_key, 6)
    for dim, parts in shards:
        draws = jnp.exp(jax.random.uniform(jax.random.fold_in(own, dim), (parts,), jnp.float32, low / len(shards), high / len(shards)))
        level = level * jnp.repeat(draws, extent[dim] // parts).reshape([-1 if axis == dim else 1 for axis in range(len(extent))])
    return level


def noise(rng, dims, scale, limit, split=(), held_as=jnp.bfloat16):
    entries = scale * jax.random.normal(rng, dims, jnp.float32)
    if split:
        entries = entries * levels(rng, dims, split, -0.22, 0.18)
    return jnp.clip(entries, -limit, limit).astype(held_as)


def setup_inputs(seed: int = 0) -> dict:
    key_list = jax.random.split(jax.random.key(seed), 8)
    sky_map = noise(key_list[0], (NRING, NPHI), 1.0, 6.0, ((0, 64), (1, 2)), jnp.float32)
    noise_weight = jnp.clip(jnp.exp(math.log(4.0) - 2.7725887 * jax.random.uniform(key_list[1], (NRING, NPHI), jnp.float32) ** levels(key_list[1], (NRING, NPHI), ((0, 64), (1, 2)), -0.2, 0.2)), 0.25, 4.0)
    prior_weight = jnp.clip(jnp.exp(math.log(4.0) - 2.0794415 * jax.random.uniform(key_list[2], (NPAIRS, NBP, 2, 128), jnp.float32) ** levels(key_list[2], (NPAIRS, NBP, 2, 128), ((0, 64), (1, 2)), -0.2, 0.2)), 0.5, 4.0)
    seeds = noise(key_list[3], (NPAIRS, NBP, 2, NRING), 1.0, 5.0, ((0, 64), (1, 2)), jnp.float32)
    loop_cos = jnp.clip(jax.random.uniform(key_list[4], (NRING,), jnp.float32, -0.3, 0.3), -0.3, 0.3)
    pair_m = set_ends(jax.random.randint(key_list[5], (NPAIRS, 2), 1, MMAX + 1), jax.random.fold_in(key_list[5], 1), 1, MMAX).astype(jnp.int32)
    block_count = draw_block_count(jax.random.fold_in(key_list[7], 71), 0)
    return dict(sky_map=sky_map, noise_weight=noise_weight, prior_weight=prior_weight, seeds=seeds, loop_cos=loop_cos, pair_m=pair_m, block_count=block_count)


EXACT = lax.Precision.HIGHEST

def block_layout(pair_m, block_count, block_ids):
    block_side = (block_ids[None, :] >= block_count[:, None]).astype(jnp.int32)
    offset = jnp.where(block_side == 0, block_ids[None, :], block_ids[None, :] - block_count[:, None])
    column_m = jnp.where(block_side == 0, pair_m[:, 0:1], pair_m[:, 1:2])
    block_start = 128 * (17 * column_m // 2048 + 1) + 128 * offset
    return (block_side, column_m, block_start)

def ladder(degree, column_m):
    degree_f = degree.astype(jnp.float32)
    m_over_l = column_m.astype(jnp.float32) / degree_f
    return jnp.sqrt((4.0 - 1.0 / (degree_f * degree_f)) / ((1.0 - m_over_l) * (1.0 + m_over_l)))

def legendre_rows(column_m, block_start, seeds, loop_cos, visit, initial):
    carried, first_out = visit(initial, seeds[:, 0], 0)
    carried, second_out = visit(carried, seeds[:, 1], 1)

    def advance(packed, step_id):
        earlier, latest, totals = packed
        degree = block_start + step_id
        coef_now = ladder(degree, column_m)[:, None]
        coef_prev = ladder(degree - 1, column_m)[:, None]
        current = coef_now * (loop_cos[None, :] * latest - earlier / coef_prev)
        totals, emitted = visit(totals, current, step_id)
        return ((latest, current, totals), emitted)
    (_, _, carried), others = lax.scan(advance, (seeds[:, 0], seeds[:, 1], carried), jnp.arange(2, 128, dtype=jnp.int32), unroll=8)
    return (carried, first_out, second_out, others)

def sum_columns(coef, block_side, column_m, block_start, seeds, loop_cos):
    pair_total, block_total = block_side.shape
    count_all = pair_total * block_total
    loop_total = loop_cos.shape[0]
    flat_coef = coef.reshape(count_all, 2, 128)

    def visit(totals, current, step_id):
        weight = lax.dynamic_index_in_dim(flat_coef, step_id, 2, keepdims=False)
        return (totals + weight[:, :, None] * current[:, None, :], None)
    totals, _, _, _ = legendre_rows(column_m.reshape(count_all), block_start.reshape(count_all), seeds.reshape(count_all, 2, loop_total), loop_cos, visit, jnp.zeros((count_all, 2, loop_total), jnp.float32))
    member = (block_side[:, :, None] == jnp.arange(2, dtype=jnp.int32)[None, None, :]).astype(jnp.float32)
    summed = jnp.einsum('pbs,pbtr->tpsr', member, totals.reshape(pair_total, block_total, 2, loop_total), precision=EXACT)
    return summed.reshape(2, 2 * pair_total, loop_total)

def spread_columns(spectra, block_side, column_m, block_start, seeds, loop_cos):
    pair_total, block_total = block_side.shape
    count_all = pair_total * block_total
    loop_total = loop_cos.shape[0]
    by_side = spectra.reshape(2, pair_total, 2, loop_total)
    side_zero = jnp.transpose(by_side[:, :, 0], (1, 0, 2))[:, None]
    side_one = jnp.transpose(by_side[:, :, 1], (1, 0, 2))[:, None]
    chosen = jnp.where(block_side[:, :, None, None] == 0, side_zero, side_one)
    flat_spec = chosen.reshape(count_all, 2, loop_total)

    def visit(carried, current, step_id):
        return (carried, lax.optimization_barrier(jnp.sum(current[:, None, :] * flat_spec, axis=2)))
    _, first_out, second_out, others = legendre_rows(column_m.reshape(count_all), block_start.reshape(count_all), seeds.reshape(count_all, 2, loop_total), loop_cos, visit, jnp.zeros((), jnp.float32))
    stacked = jnp.concatenate([first_out[None], second_out[None], others], axis=0)
    return jnp.transpose(stacked, (1, 2, 0)).reshape(pair_total, block_total, 2, 128)

def reference(sky_map, noise_weight, prior_weight, seeds, loop_cos, pair_m, block_count):
    block_side, column_m, block_start = block_layout(pair_m, block_count, jnp.arange(NBP, dtype=jnp.int32))
    every_m = pair_m.reshape(NCOL)
    map_scale = 1.0 / math.sqrt(NRING * NPHI)

    def to_map(coef):
        spectra = sum_columns(coef, block_side, column_m, block_start, seeds, loop_cos)
        values = jnp.transpose(spectra[0]) + 1j * jnp.transpose(spectra[1])
        spectrum = jnp.zeros((NRING, NPHI // 2 + 1), values.dtype).at[:, every_m].add(values)
        return jnp.fft.irfft(spectrum, n=NPHI, axis=1) * (NPHI * 0.5 * map_scale)

    def to_coef(pixels):
        spectrum = jnp.fft.rfft(pixels, axis=1)[:, every_m]
        spectra = map_scale * jnp.stack([jnp.transpose(jnp.real(spectrum)), jnp.transpose(jnp.imag(spectrum))])
        return spread_columns(spectra, block_side, column_m, block_start, seeds, loop_cos)

    def operate(coef):
        return prior_weight * coef + to_coef(noise_weight * to_map(coef))
    rhs_coef = to_coef(noise_weight * sky_map)
    solution = jnp.zeros_like(rhs_coef)
    residual = rhs_coef
    direction = rhs_coef
    norm_now = jnp.sum(residual * residual)
    for turn_id in range(ITERS):
        applied = operate(direction)
        step_len = norm_now / jnp.sum(direction * applied)
        solution = solution + step_len * direction
        residual = residual - step_len * applied
        norm_next = jnp.sum(residual * residual)
        direction = residual + norm_next / norm_now * direction
        norm_now = norm_next
    return (solution, residual)
```

```python
import functools
import math

import jax
import jax.numpy as jnp
from jax import lax
from jax.experimental import pallas as pl
from jax.experimental.pallas import tpu as pltpu
from jax.sharding import PartitionSpec as P

NPHI = 32768
NCOL = 1024
NPAIRS = 512
NBP = 4
RH = 16
CHIPS = 64
SECTION = 1024
HALF = SECTION // 2
OUTER = NPHI // SECTION
LOOPS = CHIPS * RH
GROUPS = LOOPS // 128
COARSE = 16
FINE = HALF // COARSE
SCALE = 2.0**-13
PERIOD = 2 * NPHI
F32 = jnp.float32
BF16 = jnp.bfloat16


def chip_at(group, place):
    return 8 * group + 4 * (place % 2) + place // 2


def split(value):
    high = value.astype(BF16)
    return high, (value - high.astype(F32)).astype(BF16)


def lanes(rows=8, width=128):
    return lax.broadcasted_iota(jnp.int32, (rows, width), 1)


def prepare_kernel(rep_ref, seeds_ref, cos_ref, m_ref, start_ref, keep_ref, send_ref, x_ref, step_ref, norm_ref):
    first = rep_ref[0] == 0
    low = (lanes() % 32) < 16

    def halves(near, far):
        zero = jnp.where(low, near, pltpu.roll(far, 16, 1))
        one = jnp.where(low, pltpu.roll(near, 112, 1), far)
        return jnp.where(first, zero, one), jnp.where(first, one, zero)

    for group in range(GROUPS):
        at = 256 * group
        spot = slice(128 * group, 128 * group + 128)
        near = jnp.broadcast_to(cos_ref[:, at : at + 128], (8, 128))
        far = jnp.broadcast_to(cos_ref[:, at + 128 : at + 256], (8, 128))
        x_ref[:, spot] = halves(near, far)[0]
        for block in range(2):
            for which in range(2):
                near = seeds_ref[block, which, :, at : at + 128]
                far = seeds_ref[block, which, :, at + 128 : at + 256]
                keep, send = halves(near, far)
                keep_ref[block, which, :, spot] = keep
                send_ref[block, which, :, spot] = send

    lane = lanes()

    def ladder(degree, column_m):
        ratio = column_m / degree
        return jnp.sqrt((4.0 - 1.0 / (degree * degree)) / ((1.0 - ratio) * (1.0 + ratio)))

    for block in range(NBP):
        column_m = m_ref[block].astype(F32)
        degree = start_ref[block] + lane
        now = ladder(degree.astype(F32), column_m)
        before = ladder((degree - 1).astype(F32), column_m)
        norm = jnp.where(lane < 2, 1.0, now / before)
        for shift in (2, 4, 8, 16, 32, 64):
            norm = norm * jnp.where(lane >= shift, pltpu.roll(norm, shift, 1), 1.0)
        step_ref[block] = now * pltpu.roll(norm, 1, 1) / norm
        norm_ref[block] = norm


def prepare(rep, seeds, loop_cos, column_m, block_start):
    sds = jax.ShapeDtypeStruct
    return pl.pallas_call(
        prepare_kernel,
        in_specs=[pl.BlockSpec(memory_space=pltpu.SMEM)] + [pl.BlockSpec(memory_space=pltpu.VMEM)] * 4,
        out_shape=(
            sds((2, 2, 8, LOOPS), F32),
            sds((2, 2, 8, LOOPS), F32),
            sds((8, LOOPS), F32),
            sds((NBP, 8, 128), F32),
            sds((NBP, 8, 128), F32),
        ),
        name="prepare",
    )(rep, seeds, loop_cos, column_m, block_start)


def analysis_kernel(recv_ref, seeds_ref, x_ref, step_ref, norm_ref, count_ref, out_ref, spec_ref):
    place = lanes() // 16
    tail = jnp.zeros((8, 128), F32)
    for group in range(GROUPS):
        made = [None] * 4
        for spot in range(8):
            tile = recv_ref[chip_at(group, spot)]
            tail = tail + tile
            for kind in range(4):
                turned = pltpu.roll(tile, ((spot - kind) * 16) % 128, 1) if spot != kind else tile
                made[kind] = turned if spot == 0 else jnp.where(place == spot, turned, made[kind])
        for kind in range(4):
            spec_ref[kind, group] = made[kind]
    out_ref[2 * NBP] = tail
    lane = lanes()
    even = {shift: (lane & shift) == 0 for shift in (1, 2, 4, 8, 16, 32, 64)}

    def push(stack, value, index):
        shift = 1
        while index & shift:
            first = stack.pop()
            near = jnp.where(even[shift], first, value)
            far = jnp.where(even[shift], value, first)
            value = near + pltpu.roll(far, 128 - shift, 1)
            shift *= 2
        stack.append(value)

    span = [slice(128 * g, 128 * g + 128) for g in range(GROUPS)]

    @pl.loop(0, NBP)
    def _(block):
        x = [x_ref[:, s] for s in span]
        older = [seeds_ref[block, 0, :, s] for s in span]
        newer = [seeds_ref[block, 1, :, s] for s in span]
        side = block >= count_ref[...]
        real = [jnp.where(side, spec_ref[1, g], spec_ref[0, g]) for g in range(GROUPS)]
        imag = [jnp.where(side, spec_ref[3, g], spec_ref[2, g]) for g in range(GROUPS)]
        steps = step_ref[block]

        def emit(rows, index):
            for stack, part in zip(stacks, (real, imag)):
                terms = [row * value for row, value in zip(rows, part)]
                while len(terms) > 1:
                    terms = [a + b for a, b in zip(terms[::2], terms[1::2])]
                push(stack, terms[0], index)

        stacks = ([], [])
        emit(older, 0)
        emit(newer, 1)
        for index in range(2, 128):
            factor = jnp.broadcast_to(steps[:, index : index + 1], (8, 128))
            fresh = [(factor * a) * b - c for a, b, c in zip(x, newer, older)]
            older, newer = newer, fresh
            emit(newer, index)
        outs = [stack[0] for stack in stacks]
        norm = norm_ref[block]
        out_ref[2 * block] = outs[0] * norm
        out_ref[2 * block + 1] = outs[1] * norm


def vmem(count):
    return [pl.BlockSpec(memory_space=pltpu.VMEM)] * count


def analysis(recv, seeds, x, step, norm, count):
    return pl.pallas_call(
        analysis_kernel,
        in_specs=vmem(6),
        out_shape=jax.ShapeDtypeStruct((2 * NBP + 1, 8, 128), F32),
        scratch_shapes=[pltpu.VMEM((4, GROUPS, 8, 128), F32)],
        name="analysis",
    )(recv, seeds, x, step, norm, count)


def total_of(tile):
    return jnp.sum(jnp.sum(tile, axis=1, keepdims=True), axis=0, keepdims=True)


def lane_total(tile, lane):
    return total_of(jnp.where(lanes() == lane, tile, 0.0))


def synthesis(coef_ref, seeds_ref, x_ref, step_ref, norm_ref, count_ref, spec_ref, extra, out_ref):
    span = [slice(128 * g, 128 * g + 128) for g in range(GROUPS)]
    spec_ref[...] = jnp.zeros_like(spec_ref)

    @pl.loop(0, NBP)
    def _(block):
        x = [x_ref[:, s] for s in span]
        older = [seeds_ref[block, 0, :, s] for s in span]
        newer = [seeds_ref[block, 1, :, s] for s in span]
        steps = step_ref[block]
        norm = norm_ref[block]
        real = coef_ref[2 * block] * norm
        imag = coef_ref[2 * block + 1] * norm

        def spread(values, index):
            return jnp.broadcast_to(values[:, index : index + 1], (8, 128))

        sums_re = [spread(real, 0) * a + spread(real, 1) * b for a, b in zip(older, newer)]
        sums_im = [spread(imag, 0) * a + spread(imag, 1) * b for a, b in zip(older, newer)]
        for index in range(2, 128):
            factor = spread(steps, index)
            fresh = [(factor * a) * b - c for a, b, c in zip(x, newer, older)]
            older, newer = newer, fresh
            weight_re = spread(real, index)
            weight_im = spread(imag, index)
            sums_re = [s + weight_re * p for s, p in zip(sums_re, newer)]
            sums_im = [s + weight_im * p for s, p in zip(sums_im, newer)]
        side = block >= count_ref[...]
        for g in range(GROUPS):
            spec_ref[0, g] += jnp.where(side, 0.0, sums_re[g])
            spec_ref[1, g] += jnp.where(side, sums_re[g], 0.0)
            spec_ref[2, g] += jnp.where(side, 0.0, sums_im[g])
            spec_ref[3, g] += jnp.where(side, sums_im[g], 0.0)

    place = lanes() // 16
    for group in range(GROUPS):
        values = [spec_ref[kind, group] for kind in range(4)]
        for spot in range(8):
            tile = extra
            for kind in range(4):
                turned = pltpu.roll(values[kind], ((kind - spot) * 16) % 128, 1) if spot != kind else values[kind]
                tile = jnp.where(place == kind, turned, tile)
            out_ref[chip_at(group, spot)] = tile


def first_kernel(mine_ref, other_ref, prior_ref, seeds_ref, x_ref, step_ref, norm_ref, count_ref, out_ref, rhs_ref, spec_ref):
    squares = jnp.zeros((8, 128), F32)
    energy = jnp.zeros((8, 128), F32)
    for row in range(2 * NBP):
        value = mine_ref[row] + other_ref[row]
        rhs_ref[row] = value
        squares = squares + value * value
        energy = energy + prior_ref[row] * value * value
    lane = lanes()
    extra = jnp.where(lane == 64, jnp.sum(squares, axis=1, keepdims=True), 0.0)
    extra = jnp.where(lane == 65, jnp.sum(energy, axis=1, keepdims=True), extra)
    synthesis(rhs_ref, seeds_ref, x_ref, step_ref, norm_ref, count_ref, spec_ref, extra, out_ref)


def second_kernel(
    mine_ref, other_ref, prior_ref, rhs_ref, told_ref, seeds_ref, x_ref, step_ref, norm_ref, count_ref,
    out_ref, res_ref, alpha_ref, spec_ref,
):
    told = told_ref[...]
    norm_now = lane_total(told, 0) * 0.125
    energy = lane_total(told, 1) * 0.125
    pixels = lane_total(mine_ref[2 * NBP] + other_ref[2 * NBP], 64)
    alpha = norm_now / (energy + pixels)
    alpha_ref[...] = jnp.broadcast_to(alpha, (8, 128))
    squares = jnp.zeros((8, 128), F32)
    for row in range(2 * NBP):
        image = prior_ref[row] * rhs_ref[row] + (mine_ref[row] + other_ref[row])
        value = rhs_ref[row] - alpha * image
        res_ref[row] = value
        squares = squares + value * value
    extra = jnp.where(lanes() == 64, jnp.sum(squares, axis=1, keepdims=True), 0.0)
    synthesis(res_ref, seeds_ref, x_ref, step_ref, norm_ref, count_ref, spec_ref, extra, out_ref)


def last_kernel(mine_ref, other_ref, prior_ref, rhs_ref, res_ref, dir_ref, told_ref, alpha_ref, sol_ref, out_ref):
    norm_now = lane_total(told_ref[...], 0) * 0.125
    energy = lane_total(mine_ref[2 * NBP], 65)
    pixels = lane_total(mine_ref[2 * NBP] + other_ref[2 * NBP], 64)
    alpha = norm_now / (energy + pixels)
    for row in range(2 * NBP):
        image = prior_ref[row] * dir_ref[row] + (mine_ref[row] + other_ref[row])
        sol_ref[row] = alpha_ref[...] * rhs_ref[row] + alpha * dir_ref[row]
        out_ref[row] = res_ref[row] - alpha * image


COEF = jax.ShapeDtypeStruct((2 * NBP, 8, 128), F32)
PAYLOAD = jax.ShapeDtypeStruct((CHIPS, 8, 128), F32)
TILE = jax.ShapeDtypeStruct((8, 128), F32)


def first_step(*arrays):
    return pl.pallas_call(
        first_kernel,
        in_specs=vmem(8),
        out_shape=(PAYLOAD, COEF),
        scratch_shapes=[pltpu.VMEM((4, GROUPS, 8, 128), F32)],
        name="first",
    )(*arrays)


def second_step(*arrays):
    return pl.pallas_call(
        second_kernel,
        in_specs=vmem(10),
        out_shape=(PAYLOAD, COEF, TILE),
        scratch_shapes=[pltpu.VMEM((4, GROUPS, 8, 128), F32)],
        name="second",
    )(*arrays)


def last_step(*arrays):
    return pl.pallas_call(last_kernel, in_specs=vmem(8), out_shape=(COEF, COEF), name="last")(*arrays)


ROWS = OUTER * RH
CHUNK = 256


def dot3(left, right_ref, spot):
    high, low = left
    return (
        jnp.dot(high, right_ref[0, :, spot], preferred_element_type=F32)
        + jnp.dot(low, right_ref[0, :, spot], preferred_element_type=F32)
        + jnp.dot(high, right_ref[1, :, spot], preferred_element_type=F32)
    )


def dot3_turned(left, right_ref, spot):
    high, low = left
    dims = (((1,), (1,)), ((), ()))
    return (
        lax.dot_general(high, right_ref[0, spot, :], dims, preferred_element_type=F32)
        + lax.dot_general(low, right_ref[0, spot, :], dims, preferred_element_type=F32)
        + lax.dot_general(high, right_ref[1, spot, :], dims, preferred_element_type=F32)
    )


def to_columns(even, odd, cos_ref, sin_ref, phase_ref, extra, out_ref):
    parts = [[], []]
    for at in range(0, NCOL, CHUNK):
        spot = slice(at, at + CHUNK)
        along = dot3(even, cos_ref, spot).reshape(OUTER, RH, CHUNK)
        across = dot3(odd, sin_ref, spot).reshape(OUTER, RH, CHUNK)
        real = jnp.zeros((RH, CHUNK), F32)
        imag = jnp.zeros((RH, CHUNK), F32)
        for section in range(OUTER):
            cos = phase_ref[0, section : section + 1, spot]
            sin = phase_ref[1, section : section + 1, spot]
            real = real + (cos * along[section] - sin * across[section])
            imag = imag - (cos * across[section] + sin * along[section])
        parts[0].append(real)
        parts[1].append(imag)
    rows = []
    for part in parts:
        whole = jnp.concatenate(part, axis=1)
        rows += [whole[:, :NPAIRS], whole[:, NPAIRS:]]
    whole = jnp.concatenate(rows + [extra, jnp.zeros((56, NPAIRS), F32)], axis=0)
    for at in range(0, NPAIRS, 128):
        turned = jnp.transpose(whole[:, at : at + 128])
        out_ref[at // 8 : at // 8 + 16] = turned.reshape(16, 8, 128)


def sky_kernel(
    rep_ref, noise_ref, noise_other_ref, sky_ref, sky_other_ref, angle_ref, phase_ref,
    out_ref, plus_ref, minus_ref, cos_ref, sin_ref, even_ref, odd_ref,
):
    for coarse in range(COARSE):
        c_one = angle_ref[0, coarse : coarse + 1, :]
        s_one = angle_ref[1, coarse : coarse + 1, :]
        c_two = angle_ref[0, COARSE:, :]
        s_two = angle_ref[1, COARSE:, :]
        spot = slice(FINE * coarse, FINE * coarse + FINE)
        high, low = split(c_one * c_two - s_one * s_two)
        cos_ref[0, spot, :] = high
        cos_ref[1, spot, :] = low
        high, low = split(s_one * c_two + c_one * s_two)
        sin_ref[0, spot, :] = high
        sin_ref[1, spot, :] = low
    flip = jnp.where(
        lax.broadcasted_iota(jnp.int32, (256, 256), 0) + lax.broadcasted_iota(jnp.int32, (256, 256), 1) == 255, 1.0, 0.0
    ).astype(BF16)

    def turned(rows):
        pieces = []
        for at in (256, 0):
            high, low = split(rows[:, at : at + 256])
            pieces.append(jnp.dot(high, flip, preferred_element_type=F32) + jnp.dot(low, flip, preferred_element_type=F32))
        return jnp.concatenate(pieces, axis=1)

    for half, (noise, sky) in enumerate(((noise_ref, sky_ref), (noise_other_ref, sky_other_ref))):
        count = OUTER // 2

        def rows_of(ref, offset):
            return jnp.concatenate([ref[:, SECTION * b + offset : SECTION * b + offset + HALF] for b in range(count)], axis=0)

        plus = rows_of(noise, HALF) * (SCALE * SCALE)
        minus = turned(rows_of(noise, 0)) * (SCALE * SCALE)
        spot = slice(half * count * RH, (half + 1) * count * RH)
        plus_ref[spot, :] = plus
        minus_ref[spot, :] = minus
        ahead = plus * rows_of(sky, HALF) * (1.0 / SCALE)
        back = minus * turned(rows_of(sky, 0)) * (1.0 / SCALE)
        high, low = split(ahead + back)
        even_ref[0, spot, :] = high
        even_ref[1, spot, :] = low
        high, low = split(ahead - back)
        odd_ref[0, spot, :] = high
        odd_ref[1, spot, :] = low
    to_columns(
        (even_ref[0], even_ref[1]), (odd_ref[0], odd_ref[1]), cos_ref, sin_ref, phase_ref,
        jnp.zeros((8, NPAIRS), F32), out_ref,
    )


def sky_step(rep, noise, noise_other, sky, sky_other, angles, phases):
    sds = jax.ShapeDtypeStruct
    own = pl.BlockSpec((RH, NPHI // 2), lambda i, rep: (rep[0], 0))

    def full(*shape):
        return pl.BlockSpec(shape, lambda i, rep: (0,) * len(shape))

    return pl.pallas_call(
        sky_kernel,
        grid_spec=pltpu.PrefetchScalarGridSpec(
            num_scalar_prefetch=1,
            grid=(1,),
            in_specs=[
                own, full(RH, NPHI // 2), own, full(RH, NPHI // 2),
                full(2, COARSE + FINE, NCOL), full(2, OUTER, NCOL),
            ],
            out_specs=(
                full(CHIPS, 8, 128), full(ROWS, HALF), full(ROWS, HALF),
                full(2, HALF, NCOL), full(2, HALF, NCOL),
            ),
            scratch_shapes=[pltpu.VMEM((2, ROWS, HALF), BF16), pltpu.VMEM((2, ROWS, HALF), BF16)],
        ),
        out_shape=(
            PAYLOAD, sds((ROWS, HALF), F32), sds((ROWS, HALF), F32),
            sds((2, HALF, NCOL), BF16), sds((2, HALF, NCOL), BF16),
        ),
        compiler_params=pltpu.CompilerParams(vmem_limit_bytes=60 * 2**20),
        name="sky",
    )(rep, noise, noise_other, sky, sky_other, angles, phases)


def by_rows(recv_ref):
    flat = recv_ref[...].reshape(NPAIRS, 128)
    return jnp.concatenate([jnp.transpose(flat[at : at + 128]) for at in range(0, NPAIRS, 128)], axis=1)


def through_map(rows, energy, plus_ref, minus_ref, cos_ref, sin_ref, phase_ref, out_ref, mixed_ref, even_ref, odd_ref):
    real = jnp.concatenate([rows[0:RH], rows[RH : 2 * RH]], axis=1)
    imag = jnp.concatenate([rows[2 * RH : 3 * RH], rows[3 * RH : 4 * RH]], axis=1)
    for section in range(OUTER):
        cos = phase_ref[0, section : section + 1, :]
        sin = phase_ref[1, section : section + 1, :]
        spot = slice(section * RH, section * RH + RH)
        high, low = split(real * cos - imag * sin)
        mixed_ref[0, spot, :] = high
        mixed_ref[1, spot, :] = low
        high, low = split(real * sin + imag * cos)
        mixed_ref[2, spot, :] = high
        mixed_ref[3, spot, :] = low
    power = jnp.zeros((ROWS, 128), F32)
    for at in range(0, HALF, CHUNK):
        spot = slice(at, at + CHUNK)
        even = dot3_turned((mixed_ref[0], mixed_ref[1]), cos_ref, spot)
        odd = dot3_turned((mixed_ref[2], mixed_ref[3]), sin_ref, spot)
        ahead = even - odd
        back = even + odd
        heavy_ahead = plus_ref[:, spot] * ahead
        heavy_back = minus_ref[:, spot] * back
        terms = heavy_ahead * ahead + heavy_back * back
        for piece in range(0, CHUNK, 128):
            power = power + terms[:, piece : piece + 128]
        high, low = split(heavy_ahead + heavy_back)
        even_ref[0, :, spot] = high
        even_ref[1, :, spot] = low
        high, low = split(heavy_ahead - heavy_back)
        odd_ref[0, :, spot] = high
        odd_ref[1, :, spot] = low
    pixels = total_of(power)
    lane = lanes(8, NPAIRS)
    row = lax.broadcasted_iota(jnp.int32, (8, NPAIRS), 0)
    extra = jnp.where((lane % 8 == 0) & (row == 0), pixels, 0.0)
    extra = jnp.where((lane % 8 == 0) & (row == 1), energy, extra)
    to_columns((even_ref[0], even_ref[1]), (odd_ref[0], odd_ref[1]), cos_ref, sin_ref, phase_ref, extra, out_ref)


def row_total(rows, index):
    return jnp.sum(rows[index : index + 1], axis=1, keepdims=True)


def map_one_kernel(recv_ref, plus_ref, minus_ref, cos_ref, sin_ref, phase_ref, out_ref, told_ref, mixed_ref, even_ref, odd_ref):
    rows = by_rows(recv_ref)
    lane = lanes()
    told = jnp.where(lane == 0, row_total(rows, 64), 0.0)
    told_ref[...] = jnp.where(lane == 1, row_total(rows, 65), told)
    through_map(
        rows, jnp.zeros((1, 1), F32), plus_ref, minus_ref, cos_ref, sin_ref, phase_ref, out_ref, mixed_ref, even_ref, odd_ref
    )


def map_two_kernel(
    recv_ref, before_ref, told_ref, prior_ref, rhs_ref, res_ref, plus_ref, minus_ref, cos_ref, sin_ref, phase_ref,
    out_ref, dir_ref, told_out_ref, mixed_ref, even_ref, odd_ref,
):
    rows = by_rows(recv_ref)
    norm_next = row_total(rows, 64)
    beta = norm_next / (lane_total(told_ref[...], 0) * 0.125)
    told_out_ref[...] = jnp.where(lanes() == 0, norm_next, 0.0)
    energy = jnp.zeros((8, 128), F32)
    for row in range(2 * NBP):
        value = res_ref[row] + beta * rhs_ref[row]
        dir_ref[row] = value
        energy = energy + prior_ref[row] * value * value
    rows = rows + beta * by_rows(before_ref)
    through_map(
        rows, total_of(energy), plus_ref, minus_ref, cos_ref, sin_ref, phase_ref, out_ref, mixed_ref, even_ref, odd_ref
    )


MAP_SCRATCH = [pltpu.VMEM((4, ROWS, NCOL), BF16), pltpu.VMEM((2, ROWS, HALF), BF16), pltpu.VMEM((2, ROWS, HALF), BF16)]


def map_one(*arrays):
    return pl.pallas_call(
        map_one_kernel,
        in_specs=vmem(6),
        out_shape=(PAYLOAD, TILE),
        scratch_shapes=MAP_SCRATCH,
        compiler_params=pltpu.CompilerParams(vmem_limit_bytes=60 * 2**20),
        name="map_one",
    )(*arrays)


def map_two(*arrays):
    return pl.pallas_call(
        map_two_kernel,
        in_specs=vmem(11),
        out_shape=(PAYLOAD, COEF, TILE),
        scratch_shapes=MAP_SCRATCH,
        compiler_params=pltpu.CompilerParams(vmem_limit_bytes=60 * 2**20),
        name="map_two",
    )(*arrays)


def shards(sky_map, noise_weight, prior_weight, seeds, loop_cos, pair_m, block_count):
    rep = lax.axis_index("rep")
    rep_array = jnp.reshape(rep, (1,)).astype(jnp.int32)

    def swap(value):
        return lax.ppermute(value, "rep", [(0, 1), (1, 0)])

    def both(mine, other):
        first = rep == 0
        return jnp.concatenate([jnp.where(first, mine, other), jnp.where(first, other, mine)], axis=0)

    def transpose(payload):
        return lax.all_to_all(payload, "blk", split_axis=0, concat_axis=0, tiled=True)

    away = RH * (1 - rep)
    noise_other = swap(lax.dynamic_slice_in_dim(noise_weight, away, RH, 0))
    sky_other = swap(lax.dynamic_slice_in_dim(sky_map, away, RH, 0))

    every_m = jnp.transpose(pair_m).reshape(1, NCOL)
    coarse = 2 * FINE * jnp.arange(COARSE, dtype=jnp.int32)
    fine = 2 * jnp.arange(FINE, dtype=jnp.int32) + 1
    section = jnp.arange(OUTER, dtype=jnp.int32)
    section = (section + OUTER // 2 * rep) % OUTER
    centre = 2 * SECTION * section + SECTION - 1
    factors = jnp.concatenate([coarse, fine, centre])
    cycles = factors[:, None] * every_m % PERIOD
    angles = cycles.astype(F32) * (2.0 * math.pi / PERIOD)
    table = jnp.stack([jnp.cos(angles), jnp.sin(angles)])
    inner, phases = table[:, : COARSE + FINE], table[:, COARSE + FINE :]

    local_m = lax.dynamic_slice_in_dim(pair_m, lax.axis_index("blk") * 8, 8, 0)
    blocks = jnp.arange(NBP, dtype=jnp.int32)[:, None]
    side = blocks >= block_count[None, :]
    offset = jnp.where(side, blocks - block_count[None, :], blocks)
    column_m = jnp.where(side, local_m[None, :, 1], local_m[None, :, 0])
    block_start = 128 * (17 * column_m // 2048 + 1) + 128 * offset
    wide = (NBP, 8, 128)
    count = jnp.broadcast_to(block_count[:, None], (8, 128))
    keep, send, x, step, norm = prepare(
        rep_array,
        jnp.transpose(seeds, (1, 2, 0, 3)),
        loop_cos[None, :],
        jnp.broadcast_to(column_m[:, :, None], wide),
        jnp.broadcast_to(block_start[:, :, None], wide),
    )
    seeds_all = both(keep, swap(send))
    prior_here = jnp.transpose(prior_weight, (1, 2, 0, 3))
    prior = both(prior_here, swap(prior_here)).reshape(2 * NBP, 8, 128)
    legendre = (seeds_all, x, step, norm, count)

    payload, plus, minus, cos, sin = sky_step(rep_array, noise_weight, noise_other, sky_map, sky_other, inner, phases)
    here = analysis(transpose(payload), *legendre)
    payload, rhs = first_step(here, swap(here), prior, *legendre)
    before = transpose(payload)
    payload, told = map_one(before, plus, minus, cos, sin, phases)
    here = analysis(transpose(payload), *legendre)
    payload, residual, alpha = second_step(here, swap(here), prior, rhs, told, *legendre)
    payload, direction, told = map_two(
        transpose(payload), before, told, prior, rhs, residual, plus, minus, cos, sin, phases
    )
    here = analysis(transpose(payload), *legendre)
    results = last_step(here, swap(here), prior, rhs, residual, direction, told, alpha)

    def own(value):
        part = lax.dynamic_slice_in_dim(value.reshape(NBP, 2, 8, 128), 2 * rep, 2, 0)
        return jnp.transpose(part, (2, 0, 1, 3))

    return (own(results[0]), own(results[1]))


def solution(mesh):
    placed = (
        P("blk", "rep"),
        P("blk", "rep"),
        P("blk", "rep", None, None),
        P("blk", "rep", None, None),
        P(),
        P(),
        P("blk"),
    )
    return jax.shard_map(
        shards,
        mesh=mesh,
        in_specs=placed,
        out_specs=(P("blk", "rep", None, None), P("blk", "rep", None, None)),
        check_vma=False,
    )
```

```python
import functools
import math

import jax
import jax.numpy as jnp
from jax import lax
from jax.experimental import pallas as pl
from jax.experimental.pallas import tpu as pltpu
from jax.sharding import PartitionSpec as P

NPHI = 32768
NCOL = 1024
NPAIRS = 512
NBP = 4
RH = 16
CHIPS = 64
SECTION = 1024
HALF = SECTION // 2
OUTER = NPHI // SECTION
LOOPS = CHIPS * RH
GROUPS = LOOPS // 128
COARSE = 16
FINE = HALF // COARSE
SCALE = 2.0**-13
PERIOD = 2 * NPHI
F32 = jnp.float32
BF16 = jnp.bfloat16


def chip_at(group, place):
    return 8 * group + 4 * (place % 2) + place // 2


def split(value):
    high = value.astype(BF16)
    return high, (value - high.astype(F32)).astype(BF16)


def lanes(rows=8, width=128):
    return lax.broadcasted_iota(jnp.int32, (rows, width), 1)


LIMIT = 36 * 2**20
SMEM = pl.BlockSpec(memory_space=pltpu.SMEM)
VMEM = pl.BlockSpec(memory_space=pltpu.VMEM)
COEF = pltpu.VMEM((2 * NBP, 8, 128), F32)
SPECTRA = pltpu.VMEM((2 * NBP + 1, 8, 128), F32)
PAYLOAD = pltpu.VMEM((CHIPS, 8, 128), F32)
TILE = pltpu.VMEM((8, 128), F32)
ROWS = OUTER * RH
PIXELS = jax.ShapeDtypeStruct((ROWS, HALF), F32)
TABLE = pltpu.VMEM((2, HALF, NCOL), BF16)
PHASES = pltpu.VMEM((2, OUTER, NCOL), F32)


def held(*arrays):
    return [pltpu.with_memory_space_constraint(array, pltpu.VMEM) for array in arrays]


def far(*arrays):
    return [pltpu.with_memory_space_constraint(array, pltpu.HBM) for array in arrays]


def list_of(*arrays):
    return list(arrays)


def call(kernel, outs, scratch, name, arrays, scalars=0, hold=held):
    return pl.pallas_call(
        kernel,
        in_specs=[SMEM] * scalars + [VMEM] * (len(arrays) - scalars),
        out_specs=jax.tree.map(lambda _: VMEM, outs),
        out_shape=outs,
        scratch_shapes=scratch,
        compiler_params=pltpu.CompilerParams(vmem_limit_bytes=LIMIT),
        name=name,
    )(*arrays[:scalars], *hold(*arrays[scalars:]))


WIDE = LOOPS + 128


def prepare_kernel(
    place_ref, count_ref, seeds_ref, prior_ref, cos_ref, m_ref, keep_ref, send_ref, x_ref, step_ref, norm_ref, side_ref
):
    chip, rep = place_ref[0], place_ref[1]
    first = rep == 0
    low = (lanes() % 32) < 16

    def halves(near, far):
        zero = jnp.where(low, near, pltpu.roll(far, 16, 1))
        one = jnp.where(low, pltpu.roll(near, 112, 1), far)
        return jnp.where(first, zero, one), jnp.where(first, one, zero)

    for block in range(2):
        for which in range(2):
            row = prior_ref[:, block, which, :]
            keep_ref[block, which, :, LOOPS:] = row
            send_ref[block, which, :, LOOPS:] = row
            seed = seeds_ref[:, block, which, :]
            for group in range(GROUPS):
                at = 256 * group
                spot = slice(128 * group, 128 * group + 128)
                keep, send = halves(seed[:, at : at + 128], seed[:, at + 128 : at + 256])
                keep_ref[block, which, :, spot] = keep
                send_ref[block, which, :, spot] = send
    for group in range(GROUPS):
        at = 256 * group
        near = jnp.broadcast_to(cos_ref[:, at : at + 128], (8, 128))
        far = jnp.broadcast_to(cos_ref[:, at + 128 : at + 256], (8, 128))
        x_ref[:, 128 * group : 128 * group + 128] = halves(near, far)[0]

    lane = lanes()
    row = lax.broadcasted_iota(jnp.int32, (8, NPAIRS), 0)
    chosen = lax.broadcasted_iota(jnp.int32, (8, NPAIRS), 1) == 8 * chip + row

    def own_m(side):
        every = jnp.broadcast_to(m_ref[side : side + 1, :], (8, NPAIRS)).astype(F32)
        return jnp.broadcast_to(jnp.sum(jnp.where(chosen, every, 0.0), axis=1, keepdims=True), (8, 128))

    m_zero, m_one = own_m(0).astype(jnp.int32), own_m(1).astype(jnp.int32)
    pair = lax.broadcasted_iota(jnp.int32, (8, 128), 0)
    count = jnp.zeros((8, 128), jnp.int32)
    for p in range(8):
        count = jnp.where(pair == p, count_ref[p], count)

    def ladder(degree, column_m):
        ratio = column_m / degree
        return jnp.sqrt((4.0 - 1.0 / (degree * degree)) / ((1.0 - ratio) * (1.0 + ratio)))

    for block in range(NBP):
        real_block = jnp.where(block < 2, 2 * rep + block, 2 * (1 - rep) + block - 2)
        side = real_block >= count
        m_here = jnp.where(side, m_one, m_zero)
        offset = jnp.where(side, real_block - count, real_block)
        degree = 128 * (lax.shift_right_logical(17 * m_here, 11) + 1) + 128 * offset + lane
        column_m = m_here.astype(F32)
        now = ladder(degree.astype(F32), column_m)
        before = ladder((degree - 1).astype(F32), column_m)
        norm = jnp.where(lane < 2, 1.0, now / before)
        for shift in (2, 4, 8, 16, 32, 64):
            norm = norm * jnp.where(lane >= shift, pltpu.roll(norm, shift, 1), 1.0)
        step_ref[block] = now * pltpu.roll(norm, 1, 1) / norm
        norm_ref[block] = norm
        side_ref[block] = side.astype(F32)


def prepare(*arrays):
    small = pltpu.VMEM((NBP, 8, 128), F32)
    wide = pltpu.VMEM((2, 2, 8, WIDE), F32)
    return call(prepare_kernel, (wide, wide, pltpu.VMEM((8, LOOPS), F32), small, small, small), [], "prepare", arrays, 2, list_of)


def load_seeds(keep_ref, other_ref, seeds_ref):
    seeds_ref[0:2] = keep_ref[:, :, :, :LOOPS]
    seeds_ref[2:4] = other_ref[:, :, :, :LOOPS]


def load_prior(keep_ref, other_ref):
    return [ref[j, t, :, LOOPS:] for ref in (keep_ref, other_ref) for j in range(2) for t in range(2)]


def analysis_kernel(recv_ref, keep_ref, other_ref, x_ref, step_ref, norm_ref, side_ref, out_ref, spec_ref, seeds_ref, sums_ref, halves_ref):
    load_seeds(keep_ref, other_ref, seeds_ref)
    place = lanes() // 16
    tail = jnp.zeros((8, 128), F32)
    for group in range(GROUPS):
        made = [None] * 4
        for spot in range(8):
            tile = recv_ref[chip_at(group, spot)]
            tail = tail + tile
            for kind in range(4):
                turned = pltpu.roll(tile, ((spot - kind) * 16) % 128, 1) if spot != kind else tile
                made[kind] = turned if spot == 0 else jnp.where(place == spot, turned, made[kind])
        for kind in range(4):
            spec_ref[kind, group] = made[kind]
    out_ref[2 * NBP] = tail
    lane = lanes()
    even = {shift: (lane & shift) == 0 for shift in (1, 2, 4, 8, 16, 32, 64)}

    span = [slice(128 * g, 128 * g + 128) for g in range(GROUPS)]

    @pl.loop(0, NBP)
    def _(block):
        x = [x_ref[:, s] for s in span]
        older = [seeds_ref[block, 0, :, s] for s in span]
        newer = [seeds_ref[block, 1, :, s] for s in span]
        side = side_ref[block] > 0.5
        real = [jnp.where(side, spec_ref[1, g], spec_ref[0, g]) for g in range(GROUPS)]
        imag = [jnp.where(side, spec_ref[3, g], spec_ref[2, g]) for g in range(GROUPS)]
        steps = step_ref[block]

        def emit(rows, index):
            for part, values in enumerate((real, imag)):
                terms = [row * value for row, value in zip(rows, values)]
                while len(terms) > 1:
                    terms = [a + b for a, b in zip(terms[::2], terms[1::2])]
                sums_ref[2 * block + part, index] = terms[0]

        emit(older, 0)
        emit(newer, 1)
        for index in range(2, 128):
            factor = jnp.broadcast_to(steps[:, index : index + 1], (8, 128))
            fresh = [(factor * a) * b - c for a, b, c in zip(x, newer, older)]
            older, newer = newer, fresh
            emit(newer, index)

    source, target, left = sums_ref, halves_ref, 64
    while left:
        shift = 64 // left
        for row in range(2 * NBP):
            for index in range(left):
                first, second = source[row, 2 * index], source[row, 2 * index + 1]
                near = jnp.where(even[shift], first, second)
                far = jnp.where(even[shift], second, first)
                target[row, index] = near + pltpu.roll(far, 128 - shift, 1)
        source, target, left = target, source, left // 2
    for row in range(2 * NBP):
        out_ref[row] = source[row, 0] * norm_ref[row // 2]


LEGENDRE = [pltpu.VMEM((4, GROUPS, 8, 128), F32), pltpu.VMEM((NBP, 2, 8, LOOPS), F32)]


def analysis(*arrays):
    scratch = LEGENDRE + [pltpu.VMEM((2 * NBP, count, 8, 128), F32) for count in (128, 64)]
    return call(analysis_kernel, SPECTRA, scratch, "analysis", arrays)


def total_of(tile):
    return jnp.sum(jnp.sum(tile, axis=1, keepdims=True), axis=0, keepdims=True)


def lane_total(tile, lane):
    return total_of(jnp.where(lanes() == lane, tile, 0.0))


def synthesis(coef_ref, seeds_ref, x_ref, step_ref, norm_ref, side_ref, spec_ref, extra, out_ref):
    span = [slice(128 * g, 128 * g + 128) for g in range(GROUPS)]
    spec_ref[...] = jnp.zeros_like(spec_ref)

    @pl.loop(0, NBP)
    def _(block):
        x = [x_ref[:, s] for s in span]
        older = [seeds_ref[block, 0, :, s] for s in span]
        newer = [seeds_ref[block, 1, :, s] for s in span]
        steps = step_ref[block]
        norm = norm_ref[block]
        real = coef_ref[2 * block] * norm
        imag = coef_ref[2 * block + 1] * norm

        def spread(values, index):
            return jnp.broadcast_to(values[:, index : index + 1], (8, 128))

        sums_re = [spread(real, 0) * a + spread(real, 1) * b for a, b in zip(older, newer)]
        sums_im = [spread(imag, 0) * a + spread(imag, 1) * b for a, b in zip(older, newer)]
        for index in range(2, 128):
            factor = spread(steps, index)
            fresh = [(factor * a) * b - c for a, b, c in zip(x, newer, older)]
            older, newer = newer, fresh
            weight_re = spread(real, index)
            weight_im = spread(imag, index)
            sums_re = [s + weight_re * p for s, p in zip(sums_re, newer)]
            sums_im = [s + weight_im * p for s, p in zip(sums_im, newer)]
        side = side_ref[block] > 0.5
        for g in range(GROUPS):
            spec_ref[0, g] += jnp.where(side, 0.0, sums_re[g])
            spec_ref[1, g] += jnp.where(side, sums_re[g], 0.0)
            spec_ref[2, g] += jnp.where(side, 0.0, sums_im[g])
            spec_ref[3, g] += jnp.where(side, sums_im[g], 0.0)

    place = lanes() // 16
    for group in range(GROUPS):
        values = [spec_ref[kind, group] for kind in range(4)]
        for spot in range(8):
            tile = extra
            for kind in range(4):
                turned = pltpu.roll(values[kind], ((kind - spot) * 16) % 128, 1) if spot != kind else values[kind]
                tile = jnp.where(place == kind, turned, tile)
            out_ref[chip_at(group, spot)] = tile


def swapped(row):
    return (row + NBP) % (2 * NBP)


def sum_rows(terms):
    paired = [terms[row] + terms[swapped(row)] for row in range(NBP)]
    return (paired[0] + paired[1]) + (paired[2] + paired[3])


def first_kernel(
    mine_ref, theirs_ref, keep_ref, other_ref, x_ref, step_ref, norm_ref, side_ref, out_ref, rhs_ref, spec_ref, seeds_ref
):
    load_seeds(keep_ref, other_ref, seeds_ref)
    prior = load_prior(keep_ref, other_ref)
    rhs = [mine_ref[row] + theirs_ref[swapped(row)] for row in range(2 * NBP)]
    for row in range(2 * NBP):
        rhs_ref[row] = rhs[row]
    squares = sum_rows([value * value for value in rhs])
    energy = sum_rows([weight * value * value for weight, value in zip(prior, rhs)])
    lane = lanes()
    extra = jnp.where(lane == 64, jnp.sum(squares, axis=1, keepdims=True), 0.0)
    extra = jnp.where(lane == 65, jnp.sum(energy, axis=1, keepdims=True), extra)
    synthesis(rhs_ref, seeds_ref, x_ref, step_ref, norm_ref, side_ref, spec_ref, extra, out_ref)


def second_kernel(
    mine_ref, theirs_ref, rhs_ref, told_ref, keep_ref, other_ref, x_ref, step_ref, norm_ref, side_ref,
    out_ref, res_ref, alpha_ref, spec_ref, seeds_ref,
):
    load_seeds(keep_ref, other_ref, seeds_ref)
    prior = load_prior(keep_ref, other_ref)
    told = told_ref[...]
    norm_now = lane_total(told, 0) * 0.125
    energy = lane_total(told, 1) * 0.125
    pixels = lane_total(mine_ref[2 * NBP] + theirs_ref[2 * NBP], 64)
    alpha = norm_now / (energy + pixels)
    alpha_ref[...] = jnp.broadcast_to(alpha, (8, 128))
    residual = []
    for row in range(2 * NBP):
        image = prior[row] * rhs_ref[row] + (mine_ref[row] + theirs_ref[swapped(row)])
        residual.append(rhs_ref[row] - alpha * image)
        res_ref[row] = residual[row]
    squares = sum_rows([value * value for value in residual])
    extra = jnp.where(lanes() == 64, jnp.sum(squares, axis=1, keepdims=True), 0.0)
    synthesis(res_ref, seeds_ref, x_ref, step_ref, norm_ref, side_ref, spec_ref, extra, out_ref)


def last_kernel(
    mine_ref, theirs_ref, keep_ref, rhs_ref, res_ref, dir_ref, told_ref, alpha_ref, sol_ref, out_ref
):
    norm_now = lane_total(told_ref[...], 0) * 0.125
    energy = lane_total(mine_ref[2 * NBP], 65)
    pixels = lane_total(mine_ref[2 * NBP] + theirs_ref[2 * NBP], 64)
    alpha = norm_now / (energy + pixels)
    for block in range(2):
        for part in range(2):
            row = 2 * block + part
            image = keep_ref[block, part, :, LOOPS:] * dir_ref[row] + (mine_ref[row] + theirs_ref[swapped(row)])
            sol_ref[:, block, part, :] = alpha_ref[...] * rhs_ref[row] + alpha * dir_ref[row]
            out_ref[:, block, part, :] = res_ref[row] - alpha * image


def first_step(*arrays):
    return call(first_kernel, (PAYLOAD, COEF), LEGENDRE, "first", arrays)


def second_step(*arrays):
    return call(second_kernel, (PAYLOAD, COEF, TILE), LEGENDRE, "second", arrays)


def last_step(*arrays):
    result = jax.ShapeDtypeStruct((8, 2, 2, 128), F32)
    return call(last_kernel, (result, result), [], "last", arrays)


CHUNK = 256


def dot3(left, right_ref, spot):
    high, low = left
    return (
        jnp.dot(high, right_ref[0, :, spot], preferred_element_type=F32)
        + jnp.dot(low, right_ref[0, :, spot], preferred_element_type=F32)
        + jnp.dot(high, right_ref[1, :, spot], preferred_element_type=F32)
    )


def dot3_turned(left, right_ref, spot):
    high, low = left
    dims = (((1,), (1,)), ((), ()))
    return (
        lax.dot_general(high, right_ref[0, spot, :], dims, preferred_element_type=F32)
        + lax.dot_general(low, right_ref[0, spot, :], dims, preferred_element_type=F32)
        + lax.dot_general(high, right_ref[1, spot, :], dims, preferred_element_type=F32)
    )


def to_columns(even, odd, cos_ref, sin_ref, phase_ref, extra, out_ref):
    parts = [[], []]
    for at in range(0, NCOL, CHUNK):
        spot = slice(at, at + CHUNK)
        along = dot3(even, cos_ref, spot).reshape(OUTER, RH, CHUNK)
        across = dot3(odd, sin_ref, spot).reshape(OUTER, RH, CHUNK)
        real = jnp.zeros((RH, CHUNK), F32)
        imag = jnp.zeros((RH, CHUNK), F32)
        for section in range(OUTER):
            cos = phase_ref[0, section : section + 1, spot]
            sin = phase_ref[1, section : section + 1, spot]
            real = real + (cos * along[section] - sin * across[section])
            imag = imag - (cos * across[section] + sin * along[section])
        parts[0].append(real)
        parts[1].append(imag)
    rows = []
    for part in parts:
        whole = jnp.concatenate(part, axis=1)
        rows += [whole[:, :NPAIRS], whole[:, NPAIRS:]]
    whole = jnp.concatenate(rows + [extra, jnp.zeros((56, NPAIRS), F32)], axis=0)
    for at in range(0, NPAIRS, 128):
        turned = jnp.transpose(whole[:, at : at + 128])
        out_ref[at // 8 : at // 8 + 16] = turned.reshape(16, 8, 128)


def circle(cycles):
    quarter = lax.shift_right_logical(cycles + PERIOD // 8, 14)
    angle = (cycles - quarter * (PERIOD // 4)).astype(F32) * (2.0 * math.pi / PERIOD)
    square = angle * angle
    sin = angle * (1.0 + square * (-1 / 6 + square * (1 / 120 + square * (-1 / 5040 + square * (1 / 362880)))))
    cos = 1.0 + square * (-0.5 + square * (1 / 24 + square * (-1 / 720 + square * (1 / 40320))))
    odd = (quarter & 1) == 1
    cos, sin = jnp.where(odd, sin, cos), jnp.where(odd, cos, sin)
    cos = jnp.where((quarter == 1) | (quarter == 2), -cos, cos)
    sin = jnp.where((quarter == 2) | (quarter == 3), -sin, sin)
    return cos, sin


def table_kernel(place_ref, m_ref, cos_ref, sin_ref, phase_ref):
    rep = place_ref[1]
    every_m = jnp.concatenate([m_ref[0:1, :], m_ref[1:2, :]], axis=1)

    def angles(rows, factor):
        return circle((factor(lax.broadcasted_iota(jnp.int32, (rows, NCOL), 0)) * every_m) & (PERIOD - 1))

    c_coarse, s_coarse = angles(COARSE, lambda row: 2 * FINE * row)
    c_fine, s_fine = angles(FINE, lambda row: 2 * row + 1)
    for row in range(COARSE):
        c_one, s_one = c_coarse[row : row + 1], s_coarse[row : row + 1]
        spot = slice(FINE * row, FINE * row + FINE)
        high, low = split(c_one * c_fine - s_one * s_fine)
        cos_ref[0, spot, :] = high
        cos_ref[1, spot, :] = low
        high, low = split(s_one * c_fine + c_one * s_fine)
        sin_ref[0, spot, :] = high
        sin_ref[1, spot, :] = low

    def centre(row):
        section = (row + OUTER // 2 * rep) & (OUTER - 1)
        return 2 * SECTION * section + SECTION - 1

    cos, sin = angles(OUTER, centre)
    phase_ref[0] = cos
    phase_ref[1] = sin


def tables(*arrays):
    return call(table_kernel, (TABLE, TABLE, PHASES), [], "tables", arrays, 1)


def folded(ref, offset):
    count = OUTER // 2
    return jnp.concatenate([ref[:, SECTION * b + offset : SECTION * b + offset + HALF] for b in range(count)], axis=0)


def turned(rows):
    down = lax.broadcasted_iota(jnp.int32, (256, 256), 0)
    along = lax.broadcasted_iota(jnp.int32, (256, 256), 1)
    flip = jnp.where(down + along == 255, 1.0, 0.0).astype(BF16)
    pieces = []
    for at in (256, 0):
        high, low = split(rows[:, at : at + 256])
        pieces.append(jnp.dot(high, flip, preferred_element_type=F32) + jnp.dot(low, flip, preferred_element_type=F32))
    return jnp.concatenate(pieces, axis=1)


def sky_kernel(
    rep_ref, noise_ref, sky_ref, heavy_ref, cos_ref, sin_ref, phase_ref, out_ref, even_ref, odd_ref, mine_ref
):
    mine_ref[...] = noise_ref[...] * sky_ref[...]
    for half, ref in enumerate((mine_ref, heavy_ref)):
        spot = slice(half * ROWS // 2, (half + 1) * ROWS // 2)
        ahead = folded(ref, HALF) * SCALE
        back = turned(folded(ref, 0)) * SCALE
        high, low = split(ahead + back)
        even_ref[0, spot, :] = high
        even_ref[1, spot, :] = low
        high, low = split(ahead - back)
        odd_ref[0, spot, :] = high
        odd_ref[1, spot, :] = low
    to_columns(
        (even_ref[0], even_ref[1]), (odd_ref[0], odd_ref[1]), cos_ref, sin_ref, phase_ref,
        jnp.zeros((8, NPAIRS), F32), out_ref,
    )


def noise_kernel(rep_ref, noise_ref, other_ref, plus_ref, minus_ref):
    for half, ref in enumerate((noise_ref, other_ref)):
        spot = slice(half * ROWS // 2, (half + 1) * ROWS // 2)
        plus_ref[spot, :] = folded(ref, HALF) * (SCALE * SCALE)
        minus_ref[spot, :] = turned(folded(ref, 0)) * (SCALE * SCALE)


OWN = pl.BlockSpec((RH, NPHI // 2), lambda i, rep: (rep[0], 0))


def sky_step(rep, noise, sky, heavy, cos, sin, phases):
    half = pltpu.VMEM((2, ROWS, HALF), BF16)
    return pl.pallas_call(
        sky_kernel,
        grid_spec=pltpu.PrefetchScalarGridSpec(
            num_scalar_prefetch=1,
            grid=(1,),
            in_specs=[OWN, OWN, VMEM, VMEM, VMEM, VMEM],
            out_specs=VMEM,
            scratch_shapes=[half, half, pltpu.VMEM((RH, NPHI // 2), F32)],
        ),
        out_shape=PAYLOAD,
        compiler_params=pltpu.CompilerParams(vmem_limit_bytes=LIMIT),
        name="sky",
    )(rep, *far(noise, sky), *held(heavy, cos, sin, phases))


def noise_step(rep, noise, other):
    return pl.pallas_call(
        noise_kernel,
        grid_spec=pltpu.PrefetchScalarGridSpec(
            num_scalar_prefetch=1, grid=(1,), in_specs=[OWN, VMEM], out_specs=(VMEM, VMEM)
        ),
        out_shape=(PIXELS, PIXELS),
        compiler_params=pltpu.CompilerParams(vmem_limit_bytes=LIMIT),
        name="noise",
    )(rep, *far(noise), *held(other))


def by_rows(recv_ref):
    flat = recv_ref[...].reshape(NPAIRS, 128)
    return jnp.concatenate([jnp.transpose(flat[at : at + 128]) for at in range(0, NPAIRS, 128)], axis=1)


def fetch(places, holders, sems):
    copies = [pltpu.make_async_copy(a, b, sems.at[i]) for i, (a, b) in enumerate(zip(places, holders))]
    for copy in copies:
        copy.start()
    return copies


def through_map(rows, energy, copies, holders, phase_ref, out_ref, mixed_ref, even_ref, odd_ref):
    cos_ref, sin_ref, plus_ref, minus_ref = holders
    real = jnp.concatenate([rows[0:RH], rows[RH : 2 * RH]], axis=1)
    imag = jnp.concatenate([rows[2 * RH : 3 * RH], rows[3 * RH : 4 * RH]], axis=1)
    for section in range(OUTER):
        cos = phase_ref[0, section : section + 1, :]
        sin = phase_ref[1, section : section + 1, :]
        spot = slice(section * RH, section * RH + RH)
        high, low = split(real * cos - imag * sin)
        mixed_ref[0, spot, :] = high
        mixed_ref[1, spot, :] = low
        high, low = split(real * sin + imag * cos)
        mixed_ref[2, spot, :] = high
        mixed_ref[3, spot, :] = low
    spots = [slice(at, at + CHUNK) for at in range(0, HALF, CHUNK)]
    evens = [dot3_turned((mixed_ref[0], mixed_ref[1]), cos_ref, spot) for spot in spots]
    copies[0].wait()
    odds = [dot3_turned((mixed_ref[2], mixed_ref[3]), sin_ref, spot) for spot in spots]
    copies[1].wait()
    copies[2].wait()
    power = jnp.zeros((ROWS, 128), F32)
    for spot, even, odd in zip(spots, evens, odds):
        ahead = even - odd
        back = even + odd
        heavy_ahead = plus_ref[:, spot] * ahead
        heavy_back = minus_ref[:, spot] * back
        terms = heavy_ahead * ahead + heavy_back * back
        for piece in range(0, CHUNK, 128):
            power = power + terms[:, piece : piece + 128]
        high, low = split(heavy_ahead + heavy_back)
        even_ref[0, :, spot] = high
        even_ref[1, :, spot] = low
        high, low = split(heavy_ahead - heavy_back)
        odd_ref[0, :, spot] = high
        odd_ref[1, :, spot] = low
    pixels = total_of(power)
    lane = lanes(8, NPAIRS)
    row = lax.broadcasted_iota(jnp.int32, (8, NPAIRS), 0)
    extra = jnp.where((lane % 8 == 0) & (row == 0), pixels, 0.0)
    extra = jnp.where((lane % 8 == 0) & (row == 1), energy, extra)
    to_columns((even_ref[0], even_ref[1]), (odd_ref[0], odd_ref[1]), cos_ref, sin_ref, phase_ref, extra, out_ref)


def row_total(rows, index):
    return jnp.sum(rows[index : index + 1], axis=1, keepdims=True)


def map_one_kernel(
    recv_ref, phase_ref, cos_ref, sin_hbm, plus_hbm, minus_hbm,
    out_ref, told_ref, mixed_ref, even_ref, odd_ref, sin_ref, plus_ref, minus_ref, sems,
):
    holders = (cos_ref, sin_ref, plus_ref, minus_ref)
    copies = fetch((sin_hbm, plus_hbm, minus_hbm), holders[1:], sems)
    rows = by_rows(recv_ref)
    lane = lanes()
    told = jnp.where(lane == 0, row_total(rows, 64), 0.0)
    told_ref[...] = jnp.where(lane == 1, row_total(rows, 65), told)
    through_map(rows, jnp.zeros((1, 1), F32), copies, holders, phase_ref, out_ref, mixed_ref, even_ref, odd_ref)


def map_two_kernel(
    recv_ref, before_ref, told_ref, keep_ref, other_ref, rhs_ref, res_ref, phase_ref, cos_ref, sin_hbm, plus_hbm, minus_hbm,
    out_ref, dir_ref, told_out_ref, mixed_ref, even_ref, odd_ref, sin_ref, plus_ref, minus_ref, sems,
):
    holders = (cos_ref, sin_ref, plus_ref, minus_ref)
    copies = fetch((sin_hbm, plus_hbm, minus_hbm), holders[1:], sems)
    rows = by_rows(recv_ref)
    norm_next = row_total(rows, 64)
    beta = norm_next / (lane_total(told_ref[...], 0) * 0.125)
    told_out_ref[...] = jnp.where(lanes() == 0, norm_next, 0.0)
    prior = load_prior(keep_ref, other_ref)
    terms = []
    for row in range(2 * NBP):
        value = res_ref[row] + beta * rhs_ref[row]
        dir_ref[row] = value
        terms.append(prior[row] * value * value)
    energy = sum_rows(terms)
    rows = rows + beta * by_rows(before_ref)
    through_map(rows, total_of(energy), copies, holders, phase_ref, out_ref, mixed_ref, even_ref, odd_ref)


def map_call(kernel, outs, name, arrays, tables_and_noise):
    half = pltpu.VMEM((2, ROWS, HALF), BF16)
    return pl.pallas_call(
        kernel,
        in_specs=[VMEM] * len(arrays) + [pl.BlockSpec(memory_space=pl.ANY)] * 3,
        out_specs=jax.tree.map(lambda _: VMEM, outs),
        out_shape=outs,
        scratch_shapes=[
            pltpu.VMEM((4, ROWS, NCOL), BF16), half, half,
            pltpu.VMEM((2, HALF, NCOL), BF16),
            pltpu.VMEM((ROWS, HALF), F32), pltpu.VMEM((ROWS, HALF), F32),
            pltpu.SemaphoreType.DMA((3,)),
        ],
        compiler_params=pltpu.CompilerParams(vmem_limit_bytes=LIMIT),
        name=name,
    )(*held(*arrays), *far(*tables_and_noise))


def map_one(*arrays):
    return map_call(map_one_kernel, (PAYLOAD, TILE), "map_one", arrays[:-3], arrays[-3:])


def map_two(*arrays):
    return map_call(map_two_kernel, (PAYLOAD, COEF, TILE), "map_two", arrays[:-3], arrays[-3:])


def shards(sky_map, noise_weight, prior_weight, seeds, loop_cos, pair_m, block_count):
    rep = lax.axis_index("rep")
    rep_array = jnp.reshape(rep, (1,)).astype(jnp.int32)
    place = jnp.stack([lax.axis_index("blk"), rep]).astype(jnp.int32)

    def swap(value):
        return lax.ppermute(value, "rep", [(0, 1), (1, 0)])

    def transpose(payload):
        return lax.all_to_all(payload, "blk", split_axis=0, concat_axis=0, tiled=True)

    away = RH * (1 - rep)
    noise_away = lax.dynamic_slice_in_dim(noise_weight, away, RH, 0)
    heavy = swap(noise_away * lax.dynamic_slice_in_dim(sky_map, away, RH, 0))
    every_m = jnp.transpose(pair_m)
    cos, sin, phases = tables(place, every_m)
    fourier = (cos, sin, phases)
    payload = sky_step(rep_array, noise_weight, sky_map, heavy, *fourier)
    recv = transpose(payload)

    payload, place, noise_away = lax.optimization_barrier((payload, place, noise_away))
    plus, minus = noise_step(rep_array, noise_weight, swap(noise_away))
    keep, send, x, step, norm, side = prepare(place, block_count, seeds, prior_weight, loop_cos[None, :], every_m)
    other = swap(send)
    legendre = (keep, other, x, step, norm, side)

    recv, plus, minus = lax.optimization_barrier((recv, plus, minus))
    here = analysis(recv, *legendre)
    payload, rhs = first_step(here, swap(here), *legendre)
    before = transpose(payload)
    payload, told = map_one(before, phases, cos, sin, plus, minus)
    here = analysis(transpose(payload), *legendre)
    payload, residual, alpha = second_step(here, swap(here), rhs, told, *legendre)
    payload, direction, told = map_two(
        transpose(payload), before, told, keep, other, rhs, residual, phases, cos, sin, plus, minus
    )
    here = analysis(transpose(payload), *legendre)
    return last_step(here, swap(here), keep, rhs, residual, direction, told, alpha)


def solution(mesh):
    placed = (
        P("blk", "rep"),
        P("blk", "rep"),
        P("blk", "rep", None, None),
        P("blk", "rep", None, None),
        P(),
        P(),
        P("blk"),
    )
    return jax.shard_map(
        shards,
        mesh=mesh,
        in_specs=placed,
        out_specs=(P("blk", "rep", None, None), P("blk", "rep", None, None)),
        check_vma=False,
    )
```

```python
import functools
import math

import jax
import jax.numpy as jnp
from jax import lax
from jax.experimental import pallas as pl
from jax.experimental.pallas import tpu as pltpu
from jax.sharding import PartitionSpec as P

NPHI = 32768
NCOL = 1024
NPAIRS = 512
NBP = 4
RH = 16
CHIPS = 64
SECTION = 1024
HALF = SECTION // 2
OUTER = NPHI // SECTION
LOOPS = CHIPS * RH
GROUPS = LOOPS // 128
COARSE = 16
FINE = HALF // COARSE
SCALE = 2.0**-13
PERIOD = 2 * NPHI
F32 = jnp.float32
BF16 = jnp.bfloat16


def chip_at(group, place):
    return 8 * group + 4 * (place % 2) + place // 2


def split(value):
    high = value.astype(BF16)
    return high, (value - high.astype(F32)).astype(BF16)


def lanes(rows=8, width=128):
    return lax.broadcasted_iota(jnp.int32, (rows, width), 1)


LIMIT = 36 * 2**20
SMEM = pl.BlockSpec(memory_space=pltpu.SMEM)
VMEM = pl.BlockSpec(memory_space=pltpu.VMEM)
COEF = pltpu.VMEM((2 * NBP, 8, 128), F32)
SPECTRA = pltpu.VMEM((2 * NBP + 1, 8, 128), F32)
PAYLOAD = pltpu.VMEM((CHIPS, 8, 128), F32)
TILE = pltpu.VMEM((8, 128), F32)
ROWS = OUTER * RH
PIXELS = jax.ShapeDtypeStruct((ROWS, HALF), F32)
TABLE = pltpu.VMEM((2, HALF, NCOL), BF16)
PHASES = pltpu.VMEM((2, OUTER, NCOL), F32)


def held(*arrays):
    return [pltpu.with_memory_space_constraint(array, pltpu.VMEM) for array in arrays]


def far(*arrays):
    return [pltpu.with_memory_space_constraint(array, pltpu.HBM) for array in arrays]


def list_of(*arrays):
    return list(arrays)


def call(kernel, outs, scratch, name, arrays, scalars=0, hold=held):
    return pl.pallas_call(
        kernel,
        in_specs=[SMEM] * scalars + [VMEM] * (len(arrays) - scalars),
        out_specs=jax.tree.map(lambda _: VMEM, outs),
        out_shape=outs,
        scratch_shapes=scratch,
        compiler_params=pltpu.CompilerParams(vmem_limit_bytes=LIMIT),
        name=name,
    )(*arrays[:scalars], *hold(*arrays[scalars:]))


WIDE = LOOPS + 128


def prepare_kernel(
    place_ref, count_ref, seeds_ref, prior_ref, cos_ref, m_ref, keep_ref, send_ref, x_ref, step_ref, norm_ref, side_ref
):
    chip, rep = place_ref[0], place_ref[1]
    first = rep == 0
    low = (lanes() % 32) < 16

    def halves(near, far):
        zero = jnp.where(low, near, pltpu.roll(far, 16, 1))
        one = jnp.where(low, pltpu.roll(near, 112, 1), far)
        return jnp.where(first, zero, one), jnp.where(first, one, zero)

    for block in range(2):
        for which in range(2):
            row = prior_ref[:, block, which, :]
            keep_ref[block, which, :, LOOPS:] = row
            send_ref[block, which, :, LOOPS:] = row
            seed = seeds_ref[:, block, which, :]
            for group in range(GROUPS):
                at = 256 * group
                spot = slice(128 * group, 128 * group + 128)
                keep, send = halves(seed[:, at : at + 128], seed[:, at + 128 : at + 256])
                keep_ref[block, which, :, spot] = keep
                send_ref[block, which, :, spot] = send
    for group in range(GROUPS):
        at = 256 * group
        near = jnp.broadcast_to(cos_ref[:, at : at + 128], (8, 128))
        far = jnp.broadcast_to(cos_ref[:, at + 128 : at + 256], (8, 128))
        x_ref[:, 128 * group : 128 * group + 128] = halves(near, far)[0]

    lane = lanes()
    row = lax.broadcasted_iota(jnp.int32, (8, NPAIRS), 0)
    chosen = lax.broadcasted_iota(jnp.int32, (8, NPAIRS), 1) == 8 * chip + row

    def own_m(side):
        every = jnp.broadcast_to(m_ref[side : side + 1, :], (8, NPAIRS)).astype(F32)
        return jnp.broadcast_to(jnp.sum(jnp.where(chosen, every, 0.0), axis=1, keepdims=True), (8, 128))

    m_zero, m_one = own_m(0).astype(jnp.int32), own_m(1).astype(jnp.int32)
    pair = lax.broadcasted_iota(jnp.int32, (8, 128), 0)
    count = jnp.zeros((8, 128), jnp.int32)
    for p in range(8):
        count = jnp.where(pair == p, count_ref[p], count)

    def ladder(degree, column_m):
        ratio = column_m / degree
        return jnp.sqrt((4.0 - 1.0 / (degree * degree)) / ((1.0 - ratio) * (1.0 + ratio)))

    for block in range(NBP):
        real_block = jnp.where(block < 2, 2 * rep + block, 2 * (1 - rep) + block - 2)
        side = real_block >= count
        m_here = jnp.where(side, m_one, m_zero)
        offset = jnp.where(side, real_block - count, real_block)
        degree = 128 * (lax.shift_right_logical(17 * m_here, 11) + 1) + 128 * offset + lane
        column_m = m_here.astype(F32)
        now = ladder(degree.astype(F32), column_m)
        before = ladder((degree - 1).astype(F32), column_m)
        norm = jnp.where(lane < 2, 1.0, now / before)
        for shift in (2, 4, 8, 16, 32, 64):
            norm = norm * jnp.where(lane >= shift, pltpu.roll(norm, shift, 1), 1.0)
        step_ref[block] = now * pltpu.roll(norm, 1, 1) / norm
        norm_ref[block] = norm
        side_ref[block] = side.astype(F32)


def prepare(*arrays):
    small = pltpu.VMEM((NBP, 8, 128), F32)
    wide = pltpu.VMEM((2, 2, 8, WIDE), F32)
    return call(prepare_kernel, (wide, wide, pltpu.VMEM((8, LOOPS), F32), small, small, small), [], "prepare", arrays, 2, list_of)


def load_seeds(keep_ref, other_ref, seeds_ref):
    seeds_ref[0:2] = keep_ref[:, :, :, :LOOPS]
    seeds_ref[2:4] = other_ref[:, :, :, :LOOPS]


def load_prior(keep_ref, other_ref):
    return [ref[j, t, :, LOOPS:] for ref in (keep_ref, other_ref) for j in range(2) for t in range(2)]


def analysis_kernel(recv_ref, keep_ref, other_ref, x_ref, step_ref, norm_ref, side_ref, out_ref, spec_ref, seeds_ref, sums_ref, halves_ref):
    load_seeds(keep_ref, other_ref, seeds_ref)
    place = lanes() // 16
    tail = jnp.zeros((8, 128), F32)
    for group in range(GROUPS):
        made = [None] * 4
        for spot in range(8):
            tile = recv_ref[chip_at(group, spot)]
            tail = tail + tile
            for kind in range(4):
                turned = pltpu.roll(tile, ((spot - kind) * 16) % 128, 1) if spot != kind else tile
                made[kind] = turned if spot == 0 else jnp.where(place == spot, turned, made[kind])
        for kind in range(4):
            spec_ref[kind, group] = made[kind]
    out_ref[2 * NBP] = tail
    lane = lanes()
    even = {shift: (lane & shift) == 0 for shift in (1, 2, 4, 8, 16, 32, 64)}

    span = [slice(128 * g, 128 * g + 128) for g in range(GROUPS)]

    @pl.loop(0, NBP)
    def _(block):
        x = [x_ref[:, s] for s in span]
        older = [seeds_ref[block, 0, :, s] for s in span]
        newer = [seeds_ref[block, 1, :, s] for s in span]
        side = side_ref[block] > 0.5
        real = [jnp.where(side, spec_ref[1, g], spec_ref[0, g]) for g in range(GROUPS)]
        imag = [jnp.where(side, spec_ref[3, g], spec_ref[2, g]) for g in range(GROUPS)]
        steps = step_ref[block]

        def emit(rows, index):
            for part, values in enumerate((real, imag)):
                terms = [row * value for row, value in zip(rows, values)]
                while len(terms) > 1:
                    terms = [a + b for a, b in zip(terms[::2], terms[1::2])]
                sums_ref[2 * block + part, index] = terms[0]

        emit(older, 0)
        emit(newer, 1)
        for index in range(2, 128):
            factor = jnp.broadcast_to(steps[:, index : index + 1], (8, 128))
            fresh = [(factor * a) * b - c for a, b, c in zip(x, newer, older)]
            older, newer = newer, fresh
            emit(newer, index)

    source, target, left = sums_ref, halves_ref, 64
    while left:
        shift = 64 // left
        for row in range(2 * NBP):
            for index in range(left):
                first, second = source[row, 2 * index], source[row, 2 * index + 1]
                near = jnp.where(even[shift], first, second)
                far = jnp.where(even[shift], second, first)
                target[row, index] = near + pltpu.roll(far, 128 - shift, 1)
        source, target, left = target, source, left // 2
    for row in range(2 * NBP):
        out_ref[row] = source[row, 0] * norm_ref[row // 2]


LEGENDRE = [pltpu.VMEM((4, GROUPS, 8, 128), F32), pltpu.VMEM((NBP, 2, 8, LOOPS), F32)]


def analysis(*arrays):
    scratch = LEGENDRE + [pltpu.VMEM((2 * NBP, count, 8, 128), F32) for count in (128, 64)]
    return call(analysis_kernel, SPECTRA, scratch, "analysis", arrays)


def total_of(tile):
    return jnp.sum(jnp.sum(tile, axis=1, keepdims=True), axis=0, keepdims=True)


def lane_total(tile, lane):
    return total_of(jnp.where(lanes() == lane, tile, 0.0))


def synthesis(coef_ref, seeds_ref, x_ref, step_ref, norm_ref, side_ref, spec_ref, extra, out_ref):
    span = [slice(128 * g, 128 * g + 128) for g in range(GROUPS)]
    spec_ref[...] = jnp.zeros_like(spec_ref)

    @pl.loop(0, NBP)
    def _(block):
        x = [x_ref[:, s] for s in span]
        older = [seeds_ref[block, 0, :, s] for s in span]
        newer = [seeds_ref[block, 1, :, s] for s in span]
        steps = step_ref[block]
        norm = norm_ref[block]
        real = coef_ref[2 * block] * norm
        imag = coef_ref[2 * block + 1] * norm

        def spread(values, index):
            return jnp.broadcast_to(values[:, index : index + 1], (8, 128))

        sums_re = [spread(real, 0) * a + spread(real, 1) * b for a, b in zip(older, newer)]
        sums_im = [spread(imag, 0) * a + spread(imag, 1) * b for a, b in zip(older, newer)]
        for index in range(2, 128):
            factor = spread(steps, index)
            fresh = [(factor * a) * b - c for a, b, c in zip(x, newer, older)]
            older, newer = newer, fresh
            weight_re = spread(real, index)
            weight_im = spread(imag, index)
            sums_re = [s + weight_re * p for s, p in zip(sums_re, newer)]
            sums_im = [s + weight_im * p for s, p in zip(sums_im, newer)]
        side = side_ref[block] > 0.5
        for g in range(GROUPS):
            spec_ref[0, g] += jnp.where(side, 0.0, sums_re[g])
            spec_ref[1, g] += jnp.where(side, sums_re[g], 0.0)
            spec_ref[2, g] += jnp.where(side, 0.0, sums_im[g])
            spec_ref[3, g] += jnp.where(side, sums_im[g], 0.0)

    place = lanes() // 16
    for group in range(GROUPS):
        values = [spec_ref[kind, group] for kind in range(4)]
        for spot in range(8):
            tile = extra
            for kind in range(4):
                turned = pltpu.roll(values[kind], ((kind - spot) * 16) % 128, 1) if spot != kind else values[kind]
                tile = jnp.where(place == kind, turned, tile)
            out_ref[chip_at(group, spot)] = tile


def swapped(row):
    return (row + NBP) % (2 * NBP)


def sum_rows(terms):
    paired = [terms[row] + terms[swapped(row)] for row in range(NBP)]
    return (paired[0] + paired[1]) + (paired[2] + paired[3])


def first_kernel(
    mine_ref, theirs_ref, keep_ref, other_ref, x_ref, step_ref, norm_ref, side_ref, out_ref, rhs_ref, spec_ref, seeds_ref
):
    load_seeds(keep_ref, other_ref, seeds_ref)
    prior = load_prior(keep_ref, other_ref)
    rhs = [mine_ref[row] + theirs_ref[swapped(row)] for row in range(2 * NBP)]
    for row in range(2 * NBP):
        rhs_ref[row] = rhs[row]
    squares = sum_rows([value * value for value in rhs])
    energy = sum_rows([weight * value * value for weight, value in zip(prior, rhs)])
    lane = lanes()
    extra = jnp.where(lane == 64, jnp.sum(squares, axis=1, keepdims=True), 0.0)
    extra = jnp.where(lane == 65, jnp.sum(energy, axis=1, keepdims=True), extra)
    synthesis(rhs_ref, seeds_ref, x_ref, step_ref, norm_ref, side_ref, spec_ref, extra, out_ref)


def second_kernel(
    mine_ref, theirs_ref, rhs_ref, told_ref, keep_ref, other_ref, x_ref, step_ref, norm_ref, side_ref,
    out_ref, res_ref, alpha_ref, spec_ref, seeds_ref,
):
    load_seeds(keep_ref, other_ref, seeds_ref)
    prior = load_prior(keep_ref, other_ref)
    told = told_ref[...]
    norm_now = lane_total(told, 0) * 0.125
    energy = lane_total(told, 1) * 0.125
    pixels = lane_total(mine_ref[2 * NBP] + theirs_ref[2 * NBP], 64)
    alpha = norm_now / (energy + pixels)
    alpha_ref[...] = jnp.broadcast_to(alpha, (8, 128))
    residual = []
    for row in range(2 * NBP):
        image = prior[row] * rhs_ref[row] + (mine_ref[row] + theirs_ref[swapped(row)])
        residual.append(rhs_ref[row] - alpha * image)
        res_ref[row] = residual[row]
    squares = sum_rows([value * value for value in residual])
    extra = jnp.where(lanes() == 64, jnp.sum(squares, axis=1, keepdims=True), 0.0)
    synthesis(res_ref, seeds_ref, x_ref, step_ref, norm_ref, side_ref, spec_ref, extra, out_ref)


def last_kernel(
    mine_ref, theirs_ref, keep_ref, rhs_ref, res_ref, dir_ref, told_ref, alpha_ref, sol_ref, out_ref
):
    norm_now = lane_total(told_ref[...], 0) * 0.125
    energy = lane_total(mine_ref[2 * NBP], 65)
    pixels = lane_total(mine_ref[2 * NBP] + theirs_ref[2 * NBP], 64)
    alpha = norm_now / (energy + pixels)
    for block in range(2):
        for part in range(2):
            row = 2 * block + part
            image = keep_ref[block, part, :, LOOPS:] * dir_ref[row] + (mine_ref[row] + theirs_ref[swapped(row)])
            sol_ref[:, block, part, :] = alpha_ref[...] * rhs_ref[row] + alpha * dir_ref[row]
            out_ref[:, block, part, :] = res_ref[row] - alpha * image


def first_step(*arrays):
    return call(first_kernel, (PAYLOAD, COEF), LEGENDRE, "first", arrays)


def second_step(*arrays):
    return call(second_kernel, (PAYLOAD, COEF, TILE), LEGENDRE, "second", arrays)


def last_step(*arrays):
    result = jax.ShapeDtypeStruct((8, 2, 2, 128), F32)
    return call(last_kernel, (result, result), [], "last", arrays)


CHUNK = 256


def dot3(left, right_ref, spot):
    high, low = left
    return (
        jnp.dot(high, right_ref[0, :, spot], preferred_element_type=F32)
        + jnp.dot(low, right_ref[0, :, spot], preferred_element_type=F32)
        + jnp.dot(high, right_ref[1, :, spot], preferred_element_type=F32)
    )


def dot3_turned(left, right_ref, spot):
    high, low = left
    dims = (((1,), (1,)), ((), ()))
    return (
        lax.dot_general(high, right_ref[0, spot, :], dims, preferred_element_type=F32)
        + lax.dot_general(low, right_ref[0, spot, :], dims, preferred_element_type=F32)
        + lax.dot_general(high, right_ref[1, spot, :], dims, preferred_element_type=F32)
    )


def column_sums(even, odd, first, cos_ref, sin_ref, phase_ref):
    parts = [[], []]
    count = even[0].shape[0] // RH
    for at in range(0, NCOL, CHUNK):
        spot = slice(at, at + CHUNK)
        along = dot3(even, cos_ref, spot).reshape(count, RH, CHUNK)
        across = dot3(odd, sin_ref, spot).reshape(count, RH, CHUNK)
        real = jnp.zeros((RH, CHUNK), F32)
        imag = jnp.zeros((RH, CHUNK), F32)
        for section in range(count):
            row = first + section
            cos = phase_ref[0, row : row + 1, spot]
            sin = phase_ref[1, row : row + 1, spot]
            real = real + (cos * along[section] - sin * across[section])
            imag = imag - (cos * across[section] + sin * along[section])
        parts[0].append(real)
        parts[1].append(imag)
    return [jnp.concatenate(part, axis=1) for part in parts]


def pack(parts, extra, out_ref):
    rows = []
    for whole in parts:
        rows += [whole[:, :NPAIRS], whole[:, NPAIRS:]]
    whole = jnp.concatenate(rows + [extra, jnp.zeros((56, NPAIRS), F32)], axis=0)
    for at in range(0, NPAIRS, 128):
        turned = jnp.transpose(whole[:, at : at + 128])
        out_ref[at // 8 : at // 8 + 16] = turned.reshape(16, 8, 128)


def circle(cycles):
    quarter = lax.shift_right_logical(cycles + PERIOD // 8, 14)
    angle = (cycles - quarter * (PERIOD // 4)).astype(F32) * (2.0 * math.pi / PERIOD)
    square = angle * angle
    sin = angle * (1.0 + square * (-1 / 6 + square * (1 / 120 + square * (-1 / 5040 + square * (1 / 362880)))))
    cos = 1.0 + square * (-0.5 + square * (1 / 24 + square * (-1 / 720 + square * (1 / 40320))))
    odd = (quarter & 1) == 1
    cos, sin = jnp.where(odd, sin, cos), jnp.where(odd, cos, sin)
    cos = jnp.where((quarter == 1) | (quarter == 2), -cos, cos)
    sin = jnp.where((quarter == 2) | (quarter == 3), -sin, sin)
    return cos, sin


PIECES = 4
ANY = pl.BlockSpec(memory_space=pl.ANY)


def table_kernel(
    place_ref, noise_hbm, sky_hbm, m_ref, away_ref, heavy_ref, mine_ref, cos_ref, sin_ref, phase_ref, sky_ref, noise_ref, sems
):
    rep = place_ref[1]
    width = NPHI // 2 // PIECES
    copies = []
    for half, (row, noise) in enumerate(((1 - rep, away_ref), (rep, noise_ref))):
        rows = pl.ds(pl.multiple_of(RH * row, RH), RH)
        for piece in range(PIECES):
            spot = pl.ds(piece * width, width)
            for which, (source, target) in enumerate(((noise_hbm, noise), (sky_hbm, sky_ref.at[half]))):
                sem = sems.at[half, which, piece]
                copies.append(pltpu.make_async_copy(source.at[rows, spot], target.at[:, spot], sem))
                copies[-1].start()
    every_m = jnp.concatenate([m_ref[0:1, :], m_ref[1:2, :]], axis=1)

    def angles(rows, factor):
        return circle((factor(lax.broadcasted_iota(jnp.int32, (rows, NCOL), 0)) * every_m) & (PERIOD - 1))

    c_coarse, s_coarse = angles(COARSE, lambda row: 2 * FINE * row)
    c_fine, s_fine = angles(FINE, lambda row: 2 * row + 1)
    for row in range(COARSE):
        c_one, s_one = c_coarse[row : row + 1], s_coarse[row : row + 1]
        spot = slice(FINE * row, FINE * row + FINE)
        high, low = split(c_one * c_fine - s_one * s_fine)
        cos_ref[0, spot, :] = high
        cos_ref[1, spot, :] = low
        high, low = split(s_one * c_fine + c_one * s_fine)
        sin_ref[0, spot, :] = high
        sin_ref[1, spot, :] = low

    def centre(row):
        section = (row + OUTER // 2 * rep) & (OUTER - 1)
        return 2 * SECTION * section + SECTION - 1

    cos, sin = angles(OUTER, centre)
    phase_ref[0] = cos
    phase_ref[1] = sin
    for half, (noise, out) in enumerate(((away_ref, heavy_ref), (noise_ref, mine_ref))):
        for piece in range(PIECES):
            at = 2 * (half * PIECES + piece)
            copies[at].wait()
            copies[at + 1].wait()
            spot = slice(piece * width, (piece + 1) * width)
            out[:, spot] = noise[:, spot] * sky_ref[half, :, spot]


def tables(place, noise, sky, every_m):
    pixels = pltpu.VMEM((RH, NPHI // 2), F32)
    return pl.pallas_call(
        table_kernel,
        in_specs=[SMEM, ANY, ANY, VMEM],
        out_specs=(VMEM,) * 6,
        out_shape=(pixels, pixels, pixels, TABLE, TABLE, PHASES),
        scratch_shapes=[pltpu.VMEM((2, RH, NPHI // 2), F32), pixels, pltpu.SemaphoreType.DMA((2, 2, PIECES))],
        compiler_params=pltpu.CompilerParams(vmem_limit_bytes=LIMIT),
        name="tables",
    )(place, *far(noise, sky), *held(every_m))


def folded(ref, offset):
    count = OUTER // 2
    return jnp.concatenate([ref[:, SECTION * b + offset : SECTION * b + offset + HALF] for b in range(count)], axis=0)


def turned(rows):
    down = lax.broadcasted_iota(jnp.int32, (256, 256), 0)
    along = lax.broadcasted_iota(jnp.int32, (256, 256), 1)
    flip = jnp.where(down + along == 255, 1.0, 0.0).astype(BF16)
    pieces = []
    for at in (256, 0):
        high, low = split(rows[:, at : at + 256])
        pieces.append(jnp.dot(high, flip, preferred_element_type=F32) + jnp.dot(low, flip, preferred_element_type=F32))
    return jnp.concatenate(pieces, axis=1)


def half_sums(ref, first, cos_ref, sin_ref, phase_ref):
    ahead = folded(ref, HALF) * SCALE
    back = turned(folded(ref, 0)) * SCALE
    return column_sums(split(ahead + back), split(ahead - back), first, cos_ref, sin_ref, phase_ref)


def own_kernel(mine_ref, cos_ref, sin_ref, phase_ref, sums_ref):
    sums_ref[0], sums_ref[1] = half_sums(mine_ref, 0, cos_ref, sin_ref, phase_ref)


def sky_kernel(heavy_ref, sums_ref, cos_ref, sin_ref, phase_ref, out_ref):
    parts = half_sums(heavy_ref, OUTER // 2, cos_ref, sin_ref, phase_ref)
    pack([sums_ref[0] + parts[0], sums_ref[1] + parts[1]], jnp.zeros((8, NPAIRS), F32), out_ref)


def own_step(*arrays):
    return call(own_kernel, pltpu.VMEM((2, RH, NCOL), F32), [], "own", arrays)


def sky_step(*arrays):
    return call(sky_kernel, PAYLOAD, [], "sky", arrays)


def noise_kernel(rep_ref, noise_ref, other_ref, plus_ref, minus_ref):
    for half, ref in enumerate((noise_ref, other_ref)):
        spot = slice(half * ROWS // 2, (half + 1) * ROWS // 2)
        plus_ref[spot, :] = folded(ref, HALF) * (SCALE * SCALE)
        minus_ref[spot, :] = turned(folded(ref, 0)) * (SCALE * SCALE)


OWN = pl.BlockSpec((RH, NPHI // 2), lambda i, rep: (rep[0], 0))


def noise_step(rep, noise, other):
    return pl.pallas_call(
        noise_kernel,
        grid_spec=pltpu.PrefetchScalarGridSpec(
            num_scalar_prefetch=1, grid=(1,), in_specs=[OWN, VMEM], out_specs=(VMEM, VMEM)
        ),
        out_shape=(PIXELS, PIXELS),
        compiler_params=pltpu.CompilerParams(vmem_limit_bytes=LIMIT),
        name="noise",
    )(rep, *far(noise), *held(other))


def by_rows(recv_ref):
    flat = recv_ref[...].reshape(NPAIRS, 128)
    return jnp.concatenate([jnp.transpose(flat[at : at + 128]) for at in range(0, NPAIRS, 128)], axis=1)


def fetch(places, holders, sems):
    copies = [pltpu.make_async_copy(a, b, sems.at[i]) for i, (a, b) in enumerate(zip(places, holders))]
    for copy in copies:
        copy.start()
    return copies


def through_map(rows, energy, copies, holders, phase_ref, out_ref, mixed_ref, even_ref, odd_ref):
    cos_ref, sin_ref, plus_ref, minus_ref = holders
    real = jnp.concatenate([rows[0:RH], rows[RH : 2 * RH]], axis=1)
    imag = jnp.concatenate([rows[2 * RH : 3 * RH], rows[3 * RH : 4 * RH]], axis=1)
    for section in range(OUTER):
        cos = phase_ref[0, section : section + 1, :]
        sin = phase_ref[1, section : section + 1, :]
        spot = slice(section * RH, section * RH + RH)
        high, low = split(real * cos - imag * sin)
        mixed_ref[0, spot, :] = high
        mixed_ref[1, spot, :] = low
        high, low = split(real * sin + imag * cos)
        mixed_ref[2, spot, :] = high
        mixed_ref[3, spot, :] = low
    spots = [slice(at, at + CHUNK) for at in range(0, HALF, CHUNK)]
    evens = [dot3_turned((mixed_ref[0], mixed_ref[1]), cos_ref, spot) for spot in spots]
    copies[0].wait()
    odds = [dot3_turned((mixed_ref[2], mixed_ref[3]), sin_ref, spot) for spot in spots]
    copies[1].wait()
    copies[2].wait()
    power = jnp.zeros((ROWS, 128), F32)
    for spot, even, odd in zip(spots, evens, odds):
        ahead = even - odd
        back = even + odd
        heavy_ahead = plus_ref[:, spot] * ahead
        heavy_back = minus_ref[:, spot] * back
        terms = heavy_ahead * ahead + heavy_back * back
        for piece in range(0, CHUNK, 128):
            power = power + terms[:, piece : piece + 128]
        high, low = split(heavy_ahead + heavy_back)
        even_ref[0, :, spot] = high
        even_ref[1, :, spot] = low
        high, low = split(heavy_ahead - heavy_back)
        odd_ref[0, :, spot] = high
        odd_ref[1, :, spot] = low
    pixels = total_of(power)
    lane = lanes(8, NPAIRS)
    row = lax.broadcasted_iota(jnp.int32, (8, NPAIRS), 0)
    extra = jnp.where((lane % 8 == 0) & (row == 0), pixels, 0.0)
    extra = jnp.where((lane % 8 == 0) & (row == 1), energy, extra)
    parts = column_sums((even_ref[0], even_ref[1]), (odd_ref[0], odd_ref[1]), 0, cos_ref, sin_ref, phase_ref)
    pack(parts, extra, out_ref)


def row_total(rows, index):
    return jnp.sum(rows[index : index + 1], axis=1, keepdims=True)


def map_one_kernel(
    recv_ref, phase_ref, cos_ref, sin_hbm, plus_hbm, minus_hbm,
    out_ref, told_ref, mixed_ref, even_ref, odd_ref, sin_ref, plus_ref, minus_ref, sems,
):
    holders = (cos_ref, sin_ref, plus_ref, minus_ref)
    copies = fetch((sin_hbm, plus_hbm, minus_hbm), holders[1:], sems)
    rows = by_rows(recv_ref)
    lane = lanes()
    told = jnp.where(lane == 0, row_total(rows, 64), 0.0)
    told_ref[...] = jnp.where(lane == 1, row_total(rows, 65), told)
    through_map(rows, jnp.zeros((1, 1), F32), copies, holders, phase_ref, out_ref, mixed_ref, even_ref, odd_ref)


def map_two_kernel(
    recv_ref, before_ref, told_ref, keep_ref, other_ref, rhs_ref, res_ref, phase_ref, cos_ref, sin_hbm, plus_hbm, minus_hbm,
    out_ref, dir_ref, told_out_ref, mixed_ref, even_ref, odd_ref, sin_ref, plus_ref, minus_ref, sems,
):
    holders = (cos_ref, sin_ref, plus_ref, minus_ref)
    copies = fetch((sin_hbm, plus_hbm, minus_hbm), holders[1:], sems)
    rows = by_rows(recv_ref)
    norm_next = row_total(rows, 64)
    beta = norm_next / (lane_total(told_ref[...], 0) * 0.125)
    told_out_ref[...] = jnp.where(lanes() == 0, norm_next, 0.0)
    prior = load_prior(keep_ref, other_ref)
    terms = []
    for row in range(2 * NBP):
        value = res_ref[row] + beta * rhs_ref[row]
        dir_ref[row] = value
        terms.append(prior[row] * value * value)
    energy = sum_rows(terms)
    rows = rows + beta * by_rows(before_ref)
    through_map(rows, total_of(energy), copies, holders, phase_ref, out_ref, mixed_ref, even_ref, odd_ref)


def map_call(kernel, outs, name, arrays, tables_and_noise):
    half = pltpu.VMEM((2, ROWS, HALF), BF16)
    return pl.pallas_call(
        kernel,
        in_specs=[VMEM] * len(arrays) + [ANY] * 3,
        out_specs=jax.tree.map(lambda _: VMEM, outs),
        out_shape=outs,
        scratch_shapes=[
            pltpu.VMEM((4, ROWS, NCOL), BF16), half, half,
            pltpu.VMEM((2, HALF, NCOL), BF16),
            pltpu.VMEM((ROWS, HALF), F32), pltpu.VMEM((ROWS, HALF), F32),
            pltpu.SemaphoreType.DMA((3,)),
        ],
        compiler_params=pltpu.CompilerParams(vmem_limit_bytes=LIMIT),
        name=name,
    )(*held(*arrays), *far(*tables_and_noise))


def map_one(*arrays):
    return map_call(map_one_kernel, (PAYLOAD, TILE), "map_one", arrays[:-3], arrays[-3:])


def map_two(*arrays):
    return map_call(map_two_kernel, (PAYLOAD, COEF, TILE), "map_two", arrays[:-3], arrays[-3:])


def shards(sky_map, noise_weight, prior_weight, seeds, loop_cos, pair_m, block_count):
    rep = lax.axis_index("rep")
    rep_array = jnp.reshape(rep, (1,)).astype(jnp.int32)
    place = jnp.stack([lax.axis_index("blk"), rep]).astype(jnp.int32)

    def swap(value):
        return lax.ppermute(value, "rep", [(0, 1), (1, 0)])

    def transpose(payload):
        return lax.all_to_all(payload, "blk", split_axis=0, concat_axis=0, tiled=True)

    every_m = jnp.transpose(pair_m)
    noise_away, heavy, mine, cos, sin, phases = tables(place, noise_weight, sky_map, every_m)
    heavy = swap(heavy)
    sums = own_step(mine, cos, sin, phases)
    payload = sky_step(heavy, sums, cos, sin, phases)
    recv = transpose(payload)

    payload, place, noise_away = lax.optimization_barrier((payload, place, noise_away))
    plus, minus = noise_step(rep_array, noise_weight, swap(noise_away))
    keep, send, x, step, norm, side = prepare(place, block_count, seeds, prior_weight, loop_cos[None, :], every_m)
    other = swap(send)
    legendre = (keep, other, x, step, norm, side)

    recv, plus, minus = lax.optimization_barrier((recv, plus, minus))
    here = analysis(recv, *legendre)
    payload, rhs = first_step(here, swap(here), *legendre)
    before = transpose(payload)
    payload, told = map_one(before, phases, cos, sin, plus, minus)
    here = analysis(transpose(payload), *legendre)
    payload, residual, alpha = second_step(here, swap(here), rhs, told, *legendre)
    payload, direction, told = map_two(
        transpose(payload), before, told, keep, other, rhs, residual, phases, cos, sin, plus, minus
    )
    here = analysis(transpose(payload), *legendre)
    return last_step(here, swap(here), keep, rhs, residual, direction, told, alpha)


def solution(mesh):
    placed = (
        P("blk", "rep"),
        P("blk", "rep"),
        P("blk", "rep", None, None),
        P("blk", "rep", None, None),
        P(),
        P(),
        P("blk"),
    )
    return jax.shard_map(
        shards,
        mesh=mesh,
        in_specs=placed,
        out_specs=(P("blk", "rep", None, None), P("blk", "rep", None, None)),
        check_vma=False,
    )
```

```python
import functools
import math

import jax
import jax.numpy as jnp
from jax import lax
from jax.experimental import pallas as pl
from jax.experimental.pallas import tpu as pltpu
from jax.sharding import PartitionSpec as P

NPHI = 32768
NCOL = 1024
NPAIRS = 512
NBP = 4
RH = 16
CHIPS = 64
SECTION = 1024
HALF = SECTION // 2
OUTER = NPHI // SECTION
LOOPS = CHIPS * RH
GROUPS = LOOPS // 128
COARSE = 16
FINE = HALF // COARSE
SCALE = 2.0**-13
PERIOD = 2 * NPHI
F32 = jnp.float32
BF16 = jnp.bfloat16


def chip_at(group, place):
    return 8 * group + 4 * (place % 2) + place // 2


def split(value):
    high = value.astype(BF16)
    return high, (value - high.astype(F32)).astype(BF16)


def lanes(rows=8, width=128):
    return lax.broadcasted_iota(jnp.int32, (rows, width), 1)


LIMIT = 36 * 2**20
SMEM = pl.BlockSpec(memory_space=pltpu.SMEM)
VMEM = pl.BlockSpec(memory_space=pltpu.VMEM)
COEF = pltpu.VMEM((2 * NBP, 8, 128), F32)
SPECTRA = pltpu.VMEM((2 * NBP + 1, 8, 128), F32)
PAYLOAD = pltpu.VMEM((CHIPS, 8, 128), F32)
TILE = pltpu.VMEM((8, 128), F32)
ROWS = OUTER * RH
PIXELS = jax.ShapeDtypeStruct((ROWS, HALF), F32)
TABLE = pltpu.VMEM((2, HALF, NCOL), BF16)
PHASES = pltpu.VMEM((2, OUTER, NCOL), F32)


def held(*arrays):
    return [pltpu.with_memory_space_constraint(array, pltpu.VMEM) for array in arrays]


def far(*arrays):
    return [pltpu.with_memory_space_constraint(array, pltpu.HBM) for array in arrays]


def list_of(*arrays):
    return list(arrays)


def call(kernel, outs, scratch, name, arrays, scalars=0, hold=held):
    return pl.pallas_call(
        kernel,
        in_specs=[SMEM] * scalars + [VMEM] * (len(arrays) - scalars),
        out_specs=jax.tree.map(lambda _: VMEM, outs),
        out_shape=outs,
        scratch_shapes=scratch,
        compiler_params=pltpu.CompilerParams(vmem_limit_bytes=LIMIT),
        name=name,
    )(*arrays[:scalars], *hold(*arrays[scalars:]))


WIDE = LOOPS + 128


def prepare_kernel(
    place_ref, count_ref, seeds_ref, prior_ref, cos_ref, m_ref, keep_ref, send_ref, x_ref, step_ref, norm_ref, side_ref
):
    chip, rep = place_ref[0], place_ref[1]
    first = rep == 0
    low = (lanes() % 32) < 16

    def halves(near, far):
        zero = jnp.where(low, near, pltpu.roll(far, 16, 1))
        one = jnp.where(low, pltpu.roll(near, 112, 1), far)
        return jnp.where(first, zero, one), jnp.where(first, one, zero)

    for block in range(2):
        for which in range(2):
            row = prior_ref[:, block, which, :]
            keep_ref[block, which, :, LOOPS:] = row
            send_ref[block, which, :, LOOPS:] = row
            seed = seeds_ref[:, block, which, :]
            for group in range(GROUPS):
                at = 256 * group
                spot = slice(128 * group, 128 * group + 128)
                keep, send = halves(seed[:, at : at + 128], seed[:, at + 128 : at + 256])
                keep_ref[block, which, :, spot] = keep
                send_ref[block, which, :, spot] = send
    for group in range(GROUPS):
        at = 256 * group
        near = jnp.broadcast_to(cos_ref[:, at : at + 128], (8, 128))
        far = jnp.broadcast_to(cos_ref[:, at + 128 : at + 256], (8, 128))
        x_ref[:, 128 * group : 128 * group + 128] = halves(near, far)[0]

    lane = lanes()
    row = lax.broadcasted_iota(jnp.int32, (8, NPAIRS), 0)
    chosen = lax.broadcasted_iota(jnp.int32, (8, NPAIRS), 1) == 8 * chip + row

    def own_m(side):
        every = jnp.broadcast_to(m_ref[side : side + 1, :], (8, NPAIRS)).astype(F32)
        return jnp.broadcast_to(jnp.sum(jnp.where(chosen, every, 0.0), axis=1, keepdims=True), (8, 128))

    m_zero, m_one = own_m(0).astype(jnp.int32), own_m(1).astype(jnp.int32)
    pair = lax.broadcasted_iota(jnp.int32, (8, 128), 0)
    count = jnp.zeros((8, 128), jnp.int32)
    for p in range(8):
        count = jnp.where(pair == p, count_ref[p], count)

    def ladder(degree, column_m):
        ratio = column_m / degree
        return jnp.sqrt((4.0 - 1.0 / (degree * degree)) / ((1.0 - ratio) * (1.0 + ratio)))

    for block in range(NBP):
        real_block = jnp.where(block < 2, 2 * rep + block, 2 * (1 - rep) + block - 2)
        side = real_block >= count
        m_here = jnp.where(side, m_one, m_zero)
        offset = jnp.where(side, real_block - count, real_block)
        degree = 128 * (lax.shift_right_logical(17 * m_here, 11) + 1) + 128 * offset + lane
        column_m = m_here.astype(F32)
        now = ladder(degree.astype(F32), column_m)
        before = ladder((degree - 1).astype(F32), column_m)
        norm = jnp.where(lane < 2, 1.0, now / before)
        for shift in (2, 4, 8, 16, 32, 64):
            norm = norm * jnp.where(lane >= shift, pltpu.roll(norm, shift, 1), 1.0)
        step_ref[block] = now * pltpu.roll(norm, 1, 1) / norm
        norm_ref[block] = norm
        side_ref[block] = side.astype(F32)


def prepare(*arrays):
    small = pltpu.VMEM((NBP, 8, 128), F32)
    wide = pltpu.VMEM((2, 2, 8, WIDE), F32)
    return call(prepare_kernel, (wide, wide, pltpu.VMEM((8, LOOPS), F32), small, small, small), [], "prepare", arrays, 2, list_of)


def load_seeds(keep_ref, other_ref, seeds_ref):
    seeds_ref[0:2] = keep_ref[:, :, :, :LOOPS]
    seeds_ref[2:4] = other_ref[:, :, :, :LOOPS]


def load_prior(keep_ref, other_ref):
    return [ref[j, t, :, LOOPS:] for ref in (keep_ref, other_ref) for j in range(2) for t in range(2)]


def analysis_kernel(recv_ref, keep_ref, other_ref, x_ref, step_ref, norm_ref, side_ref, out_ref, spec_ref, seeds_ref, sums_ref, halves_ref):
    load_seeds(keep_ref, other_ref, seeds_ref)
    place = lanes() // 16
    tail = jnp.zeros((8, 128), F32)
    for group in range(GROUPS):
        made = [None] * 4
        for spot in range(8):
            tile = recv_ref[chip_at(group, spot)]
            tail = tail + tile
            for kind in range(4):
                turned = pltpu.roll(tile, ((spot - kind) * 16) % 128, 1) if spot != kind else tile
                made[kind] = turned if spot == 0 else jnp.where(place == spot, turned, made[kind])
        for kind in range(4):
            spec_ref[kind, group] = made[kind]
    out_ref[2 * NBP] = tail
    lane = lanes()
    even = {shift: (lane & shift) == 0 for shift in (1, 2, 4, 8, 16, 32, 64)}

    span = [slice(128 * g, 128 * g + 128) for g in range(GROUPS)]

    @pl.loop(0, NBP)
    def _(block):
        x = [x_ref[:, s] for s in span]
        older = [seeds_ref[block, 0, :, s] for s in span]
        newer = [seeds_ref[block, 1, :, s] for s in span]
        side = side_ref[block] > 0.5
        real = [jnp.where(side, spec_ref[1, g], spec_ref[0, g]) for g in range(GROUPS)]
        imag = [jnp.where(side, spec_ref[3, g], spec_ref[2, g]) for g in range(GROUPS)]
        steps = step_ref[block]

        def emit(rows, index):
            for part, values in enumerate((real, imag)):
                terms = [row * value for row, value in zip(rows, values)]
                while len(terms) > 1:
                    terms = [a + b for a, b in zip(terms[::2], terms[1::2])]
                sums_ref[2 * block + part, index] = terms[0]

        emit(older, 0)
        emit(newer, 1)
        for index in range(2, 128):
            factor = jnp.broadcast_to(steps[:, index : index + 1], (8, 128))
            fresh = [(factor * a) * b - c for a, b, c in zip(x, newer, older)]
            older, newer = newer, fresh
            emit(newer, index)

    source, target, left = sums_ref, halves_ref, 64
    while left:
        shift = 64 // left
        for row in range(2 * NBP):
            for index in range(left):
                first, second = source[row, 2 * index], source[row, 2 * index + 1]
                near = jnp.where(even[shift], first, second)
                far = jnp.where(even[shift], second, first)
                target[row, index] = near + pltpu.roll(far, 128 - shift, 1)
        source, target, left = target, source, left // 2
    for row in range(2 * NBP):
        out_ref[row] = source[row, 0] * norm_ref[row // 2]


LEGENDRE = [pltpu.VMEM((4, GROUPS, 8, 128), F32), pltpu.VMEM((NBP, 2, 8, LOOPS), F32)]


def analysis(*arrays):
    scratch = LEGENDRE + [pltpu.VMEM((2 * NBP, count, 8, 128), F32) for count in (128, 64)]
    return call(analysis_kernel, SPECTRA, scratch, "analysis", arrays)


def total_of(tile):
    return jnp.sum(jnp.sum(tile, axis=1, keepdims=True), axis=0, keepdims=True)


def lane_total(tile, lane):
    return total_of(jnp.where(lanes() == lane, tile, 0.0))


def synthesis(coef_ref, seeds_ref, x_ref, step_ref, norm_ref, side_ref, spec_ref, extra, out_ref):
    span = [slice(128 * g, 128 * g + 128) for g in range(GROUPS)]
    spec_ref[...] = jnp.zeros_like(spec_ref)

    @pl.loop(0, NBP)
    def _(block):
        x = [x_ref[:, s] for s in span]
        older = [seeds_ref[block, 0, :, s] for s in span]
        newer = [seeds_ref[block, 1, :, s] for s in span]
        steps = step_ref[block]
        norm = norm_ref[block]
        real = coef_ref[2 * block] * norm
        imag = coef_ref[2 * block + 1] * norm

        def spread(values, index):
            return jnp.broadcast_to(values[:, index : index + 1], (8, 128))

        sums_re = [spread(real, 0) * a + spread(real, 1) * b for a, b in zip(older, newer)]
        sums_im = [spread(imag, 0) * a + spread(imag, 1) * b for a, b in zip(older, newer)]
        for index in range(2, 128):
            factor = spread(steps, index)
            fresh = [(factor * a) * b - c for a, b, c in zip(x, newer, older)]
            older, newer = newer, fresh
            weight_re = spread(real, index)
            weight_im = spread(imag, index)
            sums_re = [s + weight_re * p for s, p in zip(sums_re, newer)]
            sums_im = [s + weight_im * p for s, p in zip(sums_im, newer)]
        side = side_ref[block] > 0.5
        for g in range(GROUPS):
            spec_ref[0, g] += jnp.where(side, 0.0, sums_re[g])
            spec_ref[1, g] += jnp.where(side, sums_re[g], 0.0)
            spec_ref[2, g] += jnp.where(side, 0.0, sums_im[g])
            spec_ref[3, g] += jnp.where(side, sums_im[g], 0.0)

    place = lanes() // 16
    for group in range(GROUPS):
        values = [spec_ref[kind, group] for kind in range(4)]
        for spot in range(8):
            tile = extra
            for kind in range(4):
                turned = pltpu.roll(values[kind], ((kind - spot) * 16) % 128, 1) if spot != kind else values[kind]
                tile = jnp.where(place == kind, turned, tile)
            out_ref[chip_at(group, spot)] = tile


def swapped(row):
    return (row + NBP) % (2 * NBP)


def sum_rows(terms):
    paired = [terms[row] + terms[swapped(row)] for row in range(NBP)]
    return (paired[0] + paired[1]) + (paired[2] + paired[3])


def first_kernel(
    mine_ref, theirs_ref, keep_ref, other_ref, x_ref, step_ref, norm_ref, side_ref, out_ref, rhs_ref, spec_ref, seeds_ref
):
    load_seeds(keep_ref, other_ref, seeds_ref)
    prior = load_prior(keep_ref, other_ref)
    rhs = [mine_ref[row] + theirs_ref[swapped(row)] for row in range(2 * NBP)]
    for row in range(2 * NBP):
        rhs_ref[row] = rhs[row]
    squares = sum_rows([value * value for value in rhs])
    energy = sum_rows([weight * value * value for weight, value in zip(prior, rhs)])
    lane = lanes()
    extra = jnp.where(lane == 64, jnp.sum(squares, axis=1, keepdims=True), 0.0)
    extra = jnp.where(lane == 65, jnp.sum(energy, axis=1, keepdims=True), extra)
    synthesis(rhs_ref, seeds_ref, x_ref, step_ref, norm_ref, side_ref, spec_ref, extra, out_ref)


def second_kernel(
    mine_ref, theirs_ref, rhs_ref, told_ref, keep_ref, other_ref, x_ref, step_ref, norm_ref, side_ref,
    out_ref, res_ref, alpha_ref, spec_ref, seeds_ref,
):
    load_seeds(keep_ref, other_ref, seeds_ref)
    prior = load_prior(keep_ref, other_ref)
    told = told_ref[...]
    norm_now = lane_total(told, 0) * 0.125
    energy = lane_total(told, 1) * 0.125
    pixels = lane_total(mine_ref[2 * NBP] + theirs_ref[2 * NBP], 64)
    alpha = norm_now / (energy + pixels)
    alpha_ref[...] = jnp.broadcast_to(alpha, (8, 128))
    residual = []
    for row in range(2 * NBP):
        image = prior[row] * rhs_ref[row] + (mine_ref[row] + theirs_ref[swapped(row)])
        residual.append(rhs_ref[row] - alpha * image)
        res_ref[row] = residual[row]
    squares = sum_rows([value * value for value in residual])
    extra = jnp.where(lanes() == 64, jnp.sum(squares, axis=1, keepdims=True), 0.0)
    synthesis(res_ref, seeds_ref, x_ref, step_ref, norm_ref, side_ref, spec_ref, extra, out_ref)


def last_kernel(
    mine_ref, theirs_ref, keep_ref, rhs_ref, res_ref, dir_ref, told_ref, alpha_ref, sol_ref, out_ref
):
    norm_now = lane_total(told_ref[...], 0) * 0.125
    energy = lane_total(mine_ref[2 * NBP], 65)
    pixels = lane_total(mine_ref[2 * NBP] + theirs_ref[2 * NBP], 64)
    alpha = norm_now / (energy + pixels)
    for block in range(2):
        for part in range(2):
            row = 2 * block + part
            image = keep_ref[block, part, :, LOOPS:] * dir_ref[row] + (mine_ref[row] + theirs_ref[swapped(row)])
            sol_ref[:, block, part, :] = alpha_ref[...] * rhs_ref[row] + alpha * dir_ref[row]
            out_ref[:, block, part, :] = res_ref[row] - alpha * image


def first_step(*arrays):
    return call(first_kernel, (PAYLOAD, COEF), LEGENDRE, "first", arrays)


def second_step(*arrays):
    return call(second_kernel, (PAYLOAD, COEF, TILE), LEGENDRE, "second", arrays)


def last_step(*arrays):
    result = jax.ShapeDtypeStruct((8, 2, 2, 128), F32)
    return call(last_kernel, (result, result), [], "last", arrays)


CHUNK = 256


def dot3(left, right_ref, spot):
    high, low = left
    rows = high.shape[0]
    both = jnp.dot(jnp.concatenate([high, low], axis=0), right_ref[0, :, spot], preferred_element_type=F32)
    return both[:rows] + both[rows:] + jnp.dot(high, right_ref[1, :, spot], preferred_element_type=F32)


def dot3_turned(left, right_ref, spot):
    high, low = left
    dims = (((1,), (1,)), ((), ()))
    rows = high.shape[0]
    both = lax.dot_general(jnp.concatenate([high, low], axis=0), right_ref[0, spot, :], dims, preferred_element_type=F32)
    return both[:rows] + both[rows:] + lax.dot_general(high, right_ref[1, spot, :], dims, preferred_element_type=F32)


def column_sums(even, odd, first, cos_ref, sin_ref, phase_ref):
    parts = [[], []]
    count = even[0].shape[0] // RH
    for at in range(0, NCOL, CHUNK):
        spot = slice(at, at + CHUNK)
        along = dot3(even, cos_ref, spot).reshape(count, RH, CHUNK)
        across = dot3(odd, sin_ref, spot).reshape(count, RH, CHUNK)
        real = jnp.zeros((RH, CHUNK), F32)
        imag = jnp.zeros((RH, CHUNK), F32)
        for section in range(count):
            row = first + section
            cos = phase_ref[0, row : row + 1, spot]
            sin = phase_ref[1, row : row + 1, spot]
            real = real + (cos * along[section] - sin * across[section])
            imag = imag - (cos * across[section] + sin * along[section])
        parts[0].append(real)
        parts[1].append(imag)
    return [jnp.concatenate(part, axis=1) for part in parts]


def pack(parts, extra, out_ref):
    rows = []
    for whole in parts:
        rows += [whole[:, :NPAIRS], whole[:, NPAIRS:]]
    whole = jnp.concatenate(rows + [extra, jnp.zeros((56, NPAIRS), F32)], axis=0)
    for at in range(0, NPAIRS, 128):
        turned = jnp.transpose(whole[:, at : at + 128])
        out_ref[at // 8 : at // 8 + 16] = turned.reshape(16, 8, 128)


def circle(cycles):
    quarter = lax.shift_right_logical(cycles + PERIOD // 8, 14)
    angle = (cycles - quarter * (PERIOD // 4)).astype(F32) * (2.0 * math.pi / PERIOD)
    square = angle * angle
    sin = angle * (1.0 + square * (-1 / 6 + square * (1 / 120 + square * (-1 / 5040 + square * (1 / 362880)))))
    cos = 1.0 + square * (-0.5 + square * (1 / 24 + square * (-1 / 720 + square * (1 / 40320))))
    odd = (quarter & 1) == 1
    cos, sin = jnp.where(odd, sin, cos), jnp.where(odd, cos, sin)
    cos = jnp.where((quarter == 1) | (quarter == 2), -cos, cos)
    sin = jnp.where((quarter == 2) | (quarter == 3), -sin, sin)
    return cos, sin


PIECES = 4
ANY = pl.BlockSpec(memory_space=pl.ANY)


def table_kernel(
    place_ref, noise_hbm, sky_hbm, m_ref, away_ref, heavy_ref, mine_ref, cos_ref, sin_ref, phase_ref, sky_ref, noise_ref, sems
):
    rep = place_ref[1]
    width = NPHI // 2 // PIECES
    copies = []
    for half, (row, noise) in enumerate(((1 - rep, away_ref), (rep, noise_ref))):
        rows = pl.ds(pl.multiple_of(RH * row, RH), RH)
        for piece in range(PIECES):
            spot = pl.ds(piece * width, width)
            for which, (source, target) in enumerate(((noise_hbm, noise), (sky_hbm, sky_ref.at[half]))):
                sem = sems.at[half, which, piece]
                copies.append(pltpu.make_async_copy(source.at[rows, spot], target.at[:, spot], sem))
                copies[-1].start()
    every_m = jnp.concatenate([m_ref[0:1, :], m_ref[1:2, :]], axis=1)

    def angles(rows, factor):
        return circle((factor(lax.broadcasted_iota(jnp.int32, (rows, NCOL), 0)) * every_m) & (PERIOD - 1))

    c_coarse, s_coarse = angles(COARSE, lambda row: 2 * FINE * row)
    c_fine, s_fine = angles(FINE, lambda row: 2 * row + 1)
    for row in range(COARSE):
        c_one, s_one = c_coarse[row : row + 1], s_coarse[row : row + 1]
        spot = slice(FINE * row, FINE * row + FINE)
        high, low = split(c_one * c_fine - s_one * s_fine)
        cos_ref[0, spot, :] = high
        cos_ref[1, spot, :] = low
        high, low = split(s_one * c_fine + c_one * s_fine)
        sin_ref[0, spot, :] = high
        sin_ref[1, spot, :] = low

    def centre(row):
        section = (row + OUTER // 2 * rep) & (OUTER - 1)
        return 2 * SECTION * section + SECTION - 1

    cos, sin = angles(OUTER, centre)
    phase_ref[0] = cos
    phase_ref[1] = sin
    for half, (noise, out) in enumerate(((away_ref, heavy_ref), (noise_ref, mine_ref))):
        for piece in range(PIECES):
            at = 2 * (half * PIECES + piece)
            copies[at].wait()
            copies[at + 1].wait()
            spot = slice(piece * width, (piece + 1) * width)
            out[:, spot] = noise[:, spot] * sky_ref[half, :, spot]


def tables(place, noise, sky, every_m):
    pixels = pltpu.VMEM((RH, NPHI // 2), F32)
    return pl.pallas_call(
        table_kernel,
        in_specs=[SMEM, ANY, ANY, VMEM],
        out_specs=(VMEM,) * 6,
        out_shape=(pixels, pixels, pixels, TABLE, TABLE, PHASES),
        scratch_shapes=[pltpu.VMEM((2, RH, NPHI // 2), F32), pixels, pltpu.SemaphoreType.DMA((2, 2, PIECES))],
        compiler_params=pltpu.CompilerParams(vmem_limit_bytes=LIMIT),
        name="tables",
    )(place, *far(noise, sky), *held(every_m))


def folded(ref, offset):
    count = OUTER // 2
    return jnp.concatenate([ref[:, SECTION * b + offset : SECTION * b + offset + HALF] for b in range(count)], axis=0)


def turned(rows):
    down = lax.broadcasted_iota(jnp.int32, (256, 256), 0)
    along = lax.broadcasted_iota(jnp.int32, (256, 256), 1)
    flip = jnp.where(down + along == 255, 1.0, 0.0).astype(BF16)
    pieces = []
    for at in (256, 0):
        high, low = split(rows[:, at : at + 256])
        pieces.append(jnp.dot(high, flip, preferred_element_type=F32) + jnp.dot(low, flip, preferred_element_type=F32))
    return jnp.concatenate(pieces, axis=1)


def half_sums(ref, first, cos_ref, sin_ref, phase_ref):
    ahead = folded(ref, HALF) * SCALE
    back = turned(folded(ref, 0)) * SCALE
    return column_sums(split(ahead + back), split(ahead - back), first, cos_ref, sin_ref, phase_ref)


def own_kernel(mine_ref, cos_ref, sin_ref, phase_ref, sums_ref):
    sums_ref[0], sums_ref[1] = half_sums(mine_ref, 0, cos_ref, sin_ref, phase_ref)


def sky_kernel(heavy_ref, sums_ref, cos_ref, sin_ref, phase_ref, out_ref):
    parts = half_sums(heavy_ref, OUTER // 2, cos_ref, sin_ref, phase_ref)
    pack([sums_ref[0] + parts[0], sums_ref[1] + parts[1]], jnp.zeros((8, NPAIRS), F32), out_ref)


def own_step(*arrays):
    return call(own_kernel, pltpu.VMEM((2, RH, NCOL), F32), [], "own", arrays)


def sky_step(*arrays):
    return call(sky_kernel, PAYLOAD, [], "sky", arrays)


def noise_kernel(rep_ref, noise_ref, other_ref, plus_ref, minus_ref):
    for half, ref in enumerate((noise_ref, other_ref)):
        spot = slice(half * ROWS // 2, (half + 1) * ROWS // 2)
        plus_ref[spot, :] = folded(ref, HALF) * (SCALE * SCALE)
        minus_ref[spot, :] = turned(folded(ref, 0)) * (SCALE * SCALE)


OWN = pl.BlockSpec((RH, NPHI // 2), lambda i, rep: (rep[0], 0))


def noise_step(rep, noise, other):
    return pl.pallas_call(
        noise_kernel,
        grid_spec=pltpu.PrefetchScalarGridSpec(
            num_scalar_prefetch=1, grid=(1,), in_specs=[OWN, VMEM], out_specs=(VMEM, VMEM)
        ),
        out_shape=(PIXELS, PIXELS),
        compiler_params=pltpu.CompilerParams(vmem_limit_bytes=LIMIT),
        name="noise",
    )(rep, *far(noise), *held(other))


def by_rows(recv_ref):
    flat = recv_ref[...].reshape(NPAIRS, 128)
    return jnp.concatenate([jnp.transpose(flat[at : at + 128]) for at in range(0, NPAIRS, 128)], axis=1)


def fetch(places, holders, sems):
    copies = [pltpu.make_async_copy(a, b, sems.at[i]) for i, (a, b) in enumerate(zip(places, holders))]
    for copy in copies:
        copy.start()
    return copies


def through_map(rows, energy, copies, holders, phase_ref, out_ref, mixed_ref, even_ref, odd_ref):
    cos_ref, sin_ref, plus_ref, minus_ref = holders
    real = jnp.concatenate([rows[0:RH], rows[RH : 2 * RH]], axis=1)
    imag = jnp.concatenate([rows[2 * RH : 3 * RH], rows[3 * RH : 4 * RH]], axis=1)
    for section in range(OUTER):
        cos = phase_ref[0, section : section + 1, :]
        sin = phase_ref[1, section : section + 1, :]
        spot = slice(section * RH, section * RH + RH)
        high, low = split(real * cos - imag * sin)
        mixed_ref[0, spot, :] = high
        mixed_ref[1, spot, :] = low
        high, low = split(real * sin + imag * cos)
        mixed_ref[2, spot, :] = high
        mixed_ref[3, spot, :] = low
    spots = [slice(at, at + CHUNK) for at in range(0, HALF, CHUNK)]
    evens = [dot3_turned((mixed_ref[0], mixed_ref[1]), cos_ref, spot) for spot in spots]
    copies[0].wait()
    odds = [dot3_turned((mixed_ref[2], mixed_ref[3]), sin_ref, spot) for spot in spots]
    copies[1].wait()
    copies[2].wait()
    power = jnp.zeros((ROWS, 128), F32)
    for spot, even, odd in zip(spots, evens, odds):
        ahead = even - odd
        back = even + odd
        heavy_ahead = plus_ref[:, spot] * ahead
        heavy_back = minus_ref[:, spot] * back
        terms = heavy_ahead * ahead + heavy_back * back
        for piece in range(0, CHUNK, 128):
            power = power + terms[:, piece : piece + 128]
        high, low = split(heavy_ahead + heavy_back)
        even_ref[0, :, spot] = high
        even_ref[1, :, spot] = low
        high, low = split(heavy_ahead - heavy_back)
        odd_ref[0, :, spot] = high
        odd_ref[1, :, spot] = low
    pixels = total_of(power)
    lane = lanes(8, NPAIRS)
    row = lax.broadcasted_iota(jnp.int32, (8, NPAIRS), 0)
    extra = jnp.where((lane % 8 == 0) & (row == 0), pixels, 0.0)
    extra = jnp.where((lane % 8 == 0) & (row == 1), energy, extra)
    parts = column_sums((even_ref[0], even_ref[1]), (odd_ref[0], odd_ref[1]), 0, cos_ref, sin_ref, phase_ref)
    pack(parts, extra, out_ref)


def row_total(rows, index):
    return jnp.sum(rows[index : index + 1], axis=1, keepdims=True)


def map_one_kernel(
    recv_ref, phase_ref, cos_ref, sin_hbm, plus_hbm, minus_hbm,
    out_ref, told_ref, mixed_ref, even_ref, odd_ref, sin_ref, plus_ref, minus_ref, sems,
):
    holders = (cos_ref, sin_ref, plus_ref, minus_ref)
    copies = fetch((sin_hbm, plus_hbm, minus_hbm), holders[1:], sems)
    rows = by_rows(recv_ref)
    lane = lanes()
    told = jnp.where(lane == 0, row_total(rows, 64), 0.0)
    told_ref[...] = jnp.where(lane == 1, row_total(rows, 65), told)
    through_map(rows, jnp.zeros((1, 1), F32), copies, holders, phase_ref, out_ref, mixed_ref, even_ref, odd_ref)


def map_two_kernel(
    recv_ref, before_ref, told_ref, keep_ref, other_ref, rhs_ref, res_ref, phase_ref, cos_ref, sin_hbm, plus_hbm, minus_hbm,
    out_ref, dir_ref, told_out_ref, mixed_ref, even_ref, odd_ref, sin_ref, plus_ref, minus_ref, sems,
):
    holders = (cos_ref, sin_ref, plus_ref, minus_ref)
    copies = fetch((sin_hbm, plus_hbm, minus_hbm), holders[1:], sems)
    rows = by_rows(recv_ref)
    norm_next = row_total(rows, 64)
    beta = norm_next / (lane_total(told_ref[...], 0) * 0.125)
    told_out_ref[...] = jnp.where(lanes() == 0, norm_next, 0.0)
    prior = load_prior(keep_ref, other_ref)
    terms = []
    for row in range(2 * NBP):
        value = res_ref[row] + beta * rhs_ref[row]
        dir_ref[row] = value
        terms.append(prior[row] * value * value)
    energy = sum_rows(terms)
    rows = rows + beta * by_rows(before_ref)
    through_map(rows, total_of(energy), copies, holders, phase_ref, out_ref, mixed_ref, even_ref, odd_ref)


def map_call(kernel, outs, name, arrays, tables_and_noise):
    half = pltpu.VMEM((2, ROWS, HALF), BF16)
    return pl.pallas_call(
        kernel,
        in_specs=[VMEM] * len(arrays) + [ANY] * 3,
        out_specs=jax.tree.map(lambda _: VMEM, outs),
        out_shape=outs,
        scratch_shapes=[
            pltpu.VMEM((4, ROWS, NCOL), BF16), half, half,
            pltpu.VMEM((2, HALF, NCOL), BF16),
            pltpu.VMEM((ROWS, HALF), F32), pltpu.VMEM((ROWS, HALF), F32),
            pltpu.SemaphoreType.DMA((3,)),
        ],
        compiler_params=pltpu.CompilerParams(vmem_limit_bytes=LIMIT),
        name=name,
    )(*held(*arrays), *far(*tables_and_noise))


def map_one(*arrays):
    return map_call(map_one_kernel, (PAYLOAD, TILE), "map_one", arrays[:-3], arrays[-3:])


def map_two(*arrays):
    return map_call(map_two_kernel, (PAYLOAD, COEF, TILE), "map_two", arrays[:-3], arrays[-3:])


def shards(sky_map, noise_weight, prior_weight, seeds, loop_cos, pair_m, block_count):
    rep = lax.axis_index("rep")
    rep_array = jnp.reshape(rep, (1,)).astype(jnp.int32)
    place = jnp.stack([lax.axis_index("blk"), rep]).astype(jnp.int32)

    def swap(value):
        return lax.ppermute(value, "rep", [(0, 1), (1, 0)])

    def transpose(payload):
        return lax.all_to_all(payload, "blk", split_axis=0, concat_axis=0, tiled=True)

    every_m = jnp.transpose(pair_m)
    noise_away, heavy, mine, cos, sin, phases = tables(place, noise_weight, sky_map, every_m)
    heavy = swap(heavy)
    sums = own_step(mine, cos, sin, phases)
    payload = sky_step(heavy, sums, cos, sin, phases)
    recv = transpose(payload)

    payload, place, noise_away = lax.optimization_barrier((payload, place, noise_away))
    plus, minus = noise_step(rep_array, noise_weight, swap(noise_away))
    keep, send, x, step, norm, side = prepare(place, block_count, seeds, prior_weight, loop_cos[None, :], every_m)
    other = swap(send)
    legendre = (keep, other, x, step, norm, side)

    recv, plus, minus = lax.optimization_barrier((recv, plus, minus))
    here = analysis(recv, *legendre)
    payload, rhs = first_step(here, swap(here), *legendre)
    before = transpose(payload)
    payload, told = map_one(before, phases, cos, sin, plus, minus)
    here = analysis(transpose(payload), *legendre)
    payload, residual, alpha = second_step(here, swap(here), rhs, told, *legendre)
    payload, direction, told = map_two(
        transpose(payload), before, told, keep, other, rhs, residual, phases, cos, sin, plus, minus
    )
    here = analysis(transpose(payload), *legendre)
    return last_step(here, swap(here), keep, rhs, residual, direction, told, alpha)


def solution(mesh):
    placed = (
        P("blk", "rep"),
        P("blk", "rep"),
        P("blk", "rep", None, None),
        P("blk", "rep", None, None),
        P(),
        P(),
        P("blk"),
    )
    return jax.shard_map(
        shards,
        mesh=mesh,
        in_specs=placed,
        out_specs=(P("blk", "rep", None, None), P("blk", "rep", None, None)),
        check_vma=False,
    )
```

```python
import functools
import math

import jax
import jax.numpy as jnp
from jax import lax
from jax.experimental import pallas as pl
from jax.experimental.pallas import tpu as pltpu
from jax.sharding import PartitionSpec as P

NPHI = 32768
NCOL = 1024
NPAIRS = 512
NBP = 4
RH = 16
CHIPS = 64
SECTION = 1024
HALF = SECTION // 2
OUTER = NPHI // SECTION
LOOPS = CHIPS * RH
GROUPS = LOOPS // 128
COARSE = 16
FINE = HALF // COARSE
SCALE = 2.0**-13
PERIOD = 2 * NPHI
F32 = jnp.float32
BF16 = jnp.bfloat16


def chip_at(group, place):
    return 8 * group + 4 * (place % 2) + place // 2


def split(value):
    high = value.astype(BF16)
    return high, (value - high.astype(F32)).astype(BF16)


def lanes(rows=8, width=128):
    return lax.broadcasted_iota(jnp.int32, (rows, width), 1)


LIMIT = 36 * 2**20
SMEM = pl.BlockSpec(memory_space=pltpu.SMEM)
VMEM = pl.BlockSpec(memory_space=pltpu.VMEM)
COEF = pltpu.VMEM((2 * NBP, 8, 128), F32)
SPECTRA = pltpu.VMEM((2 * NBP + 1, 8, 128), F32)
PAYLOAD = pltpu.VMEM((CHIPS, 8, 128), F32)
TILE = pltpu.VMEM((8, 128), F32)
ROWS = OUTER * RH
PIXELS = jax.ShapeDtypeStruct((ROWS, HALF), F32)
TABLE = pltpu.VMEM((2, HALF, NCOL), BF16)
PHASES = pltpu.VMEM((2, OUTER, NCOL), F32)


def held(*arrays):
    return [pltpu.with_memory_space_constraint(array, pltpu.VMEM) for array in arrays]


def far(*arrays):
    return [pltpu.with_memory_space_constraint(array, pltpu.HBM) for array in arrays]


def list_of(*arrays):
    return list(arrays)


def call(kernel, outs, scratch, name, arrays, scalars=0, hold=held):
    return pl.pallas_call(
        kernel,
        in_specs=[SMEM] * scalars + [VMEM] * (len(arrays) - scalars),
        out_specs=jax.tree.map(lambda _: VMEM, outs),
        out_shape=outs,
        scratch_shapes=scratch,
        compiler_params=pltpu.CompilerParams(vmem_limit_bytes=LIMIT),
        name=name,
    )(*arrays[:scalars], *hold(*arrays[scalars:]))


WIDE = LOOPS + 128


def prepare_kernel(
    place_ref, count_ref, seeds_ref, prior_ref, cos_ref, m_ref, keep_ref, send_ref, x_ref, step_ref, norm_ref, side_ref
):
    chip, rep = place_ref[0], place_ref[1]
    first = rep == 0
    low = (lanes() % 32) < 16

    def halves(near, far):
        zero = jnp.where(low, near, pltpu.roll(far, 16, 1))
        one = jnp.where(low, pltpu.roll(near, 112, 1), far)
        return jnp.where(first, zero, one), jnp.where(first, one, zero)

    for block in range(2):
        for which in range(2):
            row = prior_ref[:, block, which, :]
            keep_ref[block, which, :, LOOPS:] = row
            send_ref[block, which, :, LOOPS:] = row
            seed = seeds_ref[:, block, which, :]
            for group in range(GROUPS):
                at = 256 * group
                spot = slice(128 * group, 128 * group + 128)
                keep, send = halves(seed[:, at : at + 128], seed[:, at + 128 : at + 256])
                keep_ref[block, which, :, spot] = keep
                send_ref[block, which, :, spot] = send
    for group in range(GROUPS):
        at = 256 * group
        near = jnp.broadcast_to(cos_ref[:, at : at + 128], (8, 128))
        far = jnp.broadcast_to(cos_ref[:, at + 128 : at + 256], (8, 128))
        x_ref[:, 128 * group : 128 * group + 128] = halves(near, far)[0]

    lane = lanes()
    row = lax.broadcasted_iota(jnp.int32, (8, NPAIRS), 0)
    chosen = lax.broadcasted_iota(jnp.int32, (8, NPAIRS), 1) == 8 * chip + row

    def own_m(side):
        every = jnp.broadcast_to(m_ref[side : side + 1, :], (8, NPAIRS)).astype(F32)
        return jnp.broadcast_to(jnp.sum(jnp.where(chosen, every, 0.0), axis=1, keepdims=True), (8, 128))

    m_zero, m_one = own_m(0).astype(jnp.int32), own_m(1).astype(jnp.int32)
    pair = lax.broadcasted_iota(jnp.int32, (8, 128), 0)
    count = jnp.zeros((8, 128), jnp.int32)
    for p in range(8):
        count = jnp.where(pair == p, count_ref[p], count)

    def ladder(degree, column_m):
        ratio = column_m / degree
        return jnp.sqrt((4.0 - 1.0 / (degree * degree)) / ((1.0 - ratio) * (1.0 + ratio)))

    for block in range(NBP):
        real_block = jnp.where(block < 2, 2 * rep + block, 2 * (1 - rep) + block - 2)
        side = real_block >= count
        m_here = jnp.where(side, m_one, m_zero)
        offset = jnp.where(side, real_block - count, real_block)
        degree = 128 * (lax.shift_right_logical(17 * m_here, 11) + 1) + 128 * offset + lane
        column_m = m_here.astype(F32)
        now = ladder(degree.astype(F32), column_m)
        before = ladder((degree - 1).astype(F32), column_m)
        norm = jnp.where(lane < 2, 1.0, now / before)
        for shift in (2, 4, 8, 16, 32, 64):
            norm = norm * jnp.where(lane >= shift, pltpu.roll(norm, shift, 1), 1.0)
        step_ref[block] = now * pltpu.roll(norm, 1, 1) / norm
        norm_ref[block] = norm
        side_ref[block] = side.astype(F32)


def prepare(*arrays):
    small = pltpu.VMEM((NBP, 8, 128), F32)
    wide = pltpu.VMEM((2, 2, 8, WIDE), F32)
    return call(prepare_kernel, (wide, wide, pltpu.VMEM((8, LOOPS), F32), small, small, small), [], "prepare", arrays, 2, list_of)


def load_seeds(keep_ref, other_ref, seeds_ref):
    seeds_ref[0:2] = keep_ref[:, :, :, :LOOPS]
    seeds_ref[2:4] = other_ref[:, :, :, :LOOPS]


def load_prior(keep_ref, other_ref):
    return [ref[j, t, :, LOOPS:] for ref in (keep_ref, other_ref) for j in range(2) for t in range(2)]


def analysis_kernel(recv_ref, keep_ref, other_ref, x_ref, step_ref, norm_ref, side_ref, out_ref, spec_ref, seeds_ref, sums_ref, halves_ref):
    load_seeds(keep_ref, other_ref, seeds_ref)
    place = lanes() // 16
    tail = jnp.zeros((8, 128), F32)
    for group in range(GROUPS):
        made = [None] * 4
        for spot in range(8):
            tile = recv_ref[chip_at(group, spot)]
            tail = tail + tile
            for kind in range(4):
                turned = pltpu.roll(tile, ((spot - kind) * 16) % 128, 1) if spot != kind else tile
                made[kind] = turned if spot == 0 else jnp.where(place == spot, turned, made[kind])
        for kind in range(4):
            spec_ref[kind, group] = made[kind]
    out_ref[2 * NBP] = tail
    lane = lanes()
    even = {shift: (lane & shift) == 0 for shift in (1, 2, 4, 8, 16, 32, 64)}

    span = [slice(128 * g, 128 * g + 128) for g in range(GROUPS)]

    @pl.loop(0, NBP)
    def _(block):
        x = [x_ref[:, s] for s in span]
        older = [seeds_ref[block, 0, :, s] for s in span]
        newer = [seeds_ref[block, 1, :, s] for s in span]
        side = side_ref[block] > 0.5
        real = [jnp.where(side, spec_ref[1, g], spec_ref[0, g]) for g in range(GROUPS)]
        imag = [jnp.where(side, spec_ref[3, g], spec_ref[2, g]) for g in range(GROUPS)]
        steps = step_ref[block]

        def emit(rows, index):
            for part, values in enumerate((real, imag)):
                terms = [row * value for row, value in zip(rows, values)]
                while len(terms) > 1:
                    terms = [a + b for a, b in zip(terms[::2], terms[1::2])]
                sums_ref[2 * block + part, index] = terms[0]

        emit(older, 0)
        emit(newer, 1)
        for index in range(2, 128):
            factor = jnp.broadcast_to(steps[:, index : index + 1], (8, 128))
            fresh = [(factor * a) * b - c for a, b, c in zip(x, newer, older)]
            older, newer = newer, fresh
            emit(newer, index)

    source, target, left = sums_ref, halves_ref, 64
    while left:
        shift = 64 // left
        for row in range(2 * NBP):
            for index in range(left):
                first, second = source[row, 2 * index], source[row, 2 * index + 1]
                near = jnp.where(even[shift], first, second)
                far = jnp.where(even[shift], second, first)
                target[row, index] = near + pltpu.roll(far, 128 - shift, 1)
        source, target, left = target, source, left // 2
    for row in range(2 * NBP):
        out_ref[row] = source[row, 0] * norm_ref[row // 2]


LEGENDRE = [pltpu.VMEM((4, GROUPS, 8, 128), F32), pltpu.VMEM((NBP, 2, 8, LOOPS), F32)]


def analysis(*arrays):
    scratch = LEGENDRE + [pltpu.VMEM((2 * NBP, count, 8, 128), F32) for count in (128, 64)]
    return call(analysis_kernel, SPECTRA, scratch, "analysis", arrays)


def total_of(tile):
    return jnp.sum(jnp.sum(tile, axis=1, keepdims=True), axis=0, keepdims=True)


def lane_total(tile, lane):
    return total_of(jnp.where(lanes() == lane, tile, 0.0))


def synthesis(coef_ref, seeds_ref, x_ref, step_ref, norm_ref, side_ref, spec_ref, extra, out_ref):
    span = [slice(128 * g, 128 * g + 128) for g in range(GROUPS)]
    spec_ref[...] = jnp.zeros_like(spec_ref)

    @pl.loop(0, NBP)
    def _(block):
        x = [x_ref[:, s] for s in span]
        older = [seeds_ref[block, 0, :, s] for s in span]
        newer = [seeds_ref[block, 1, :, s] for s in span]
        steps = step_ref[block]
        norm = norm_ref[block]
        real = coef_ref[2 * block] * norm
        imag = coef_ref[2 * block + 1] * norm

        def spread(values, index):
            return jnp.broadcast_to(values[:, index : index + 1], (8, 128))

        sums_re = [spread(real, 0) * a + spread(real, 1) * b for a, b in zip(older, newer)]
        sums_im = [spread(imag, 0) * a + spread(imag, 1) * b for a, b in zip(older, newer)]
        for index in range(2, 128):
            factor = spread(steps, index)
            fresh = [(factor * a) * b - c for a, b, c in zip(x, newer, older)]
            older, newer = newer, fresh
            weight_re = spread(real, index)
            weight_im = spread(imag, index)
            sums_re = [s + weight_re * p for s, p in zip(sums_re, newer)]
            sums_im = [s + weight_im * p for s, p in zip(sums_im, newer)]
        side = side_ref[block] > 0.5
        for g in range(GROUPS):
            spec_ref[0, g] += jnp.where(side, 0.0, sums_re[g])
            spec_ref[1, g] += jnp.where(side, sums_re[g], 0.0)
            spec_ref[2, g] += jnp.where(side, 0.0, sums_im[g])
            spec_ref[3, g] += jnp.where(side, sums_im[g], 0.0)

    place = lanes() // 16
    for group in range(GROUPS):
        values = [spec_ref[kind, group] for kind in range(4)]
        for spot in range(8):
            tile = extra
            for kind in range(4):
                turned = pltpu.roll(values[kind], ((kind - spot) * 16) % 128, 1) if spot != kind else values[kind]
                tile = jnp.where(place == kind, turned, tile)
            out_ref[chip_at(group, spot)] = tile


def swapped(row):
    return (row + NBP) % (2 * NBP)


def sum_rows(terms):
    paired = [terms[row] + terms[swapped(row)] for row in range(NBP)]
    return (paired[0] + paired[1]) + (paired[2] + paired[3])


def first_kernel(
    mine_ref, theirs_ref, keep_ref, other_ref, x_ref, step_ref, norm_ref, side_ref, out_ref, rhs_ref, spec_ref, seeds_ref
):
    load_seeds(keep_ref, other_ref, seeds_ref)
    prior = load_prior(keep_ref, other_ref)
    rhs = [mine_ref[row] + theirs_ref[swapped(row)] for row in range(2 * NBP)]
    for row in range(2 * NBP):
        rhs_ref[row] = rhs[row]
    squares = sum_rows([value * value for value in rhs])
    energy = sum_rows([weight * value * value for weight, value in zip(prior, rhs)])
    lane = lanes()
    extra = jnp.where(lane == 64, jnp.sum(squares, axis=1, keepdims=True), 0.0)
    extra = jnp.where(lane == 65, jnp.sum(energy, axis=1, keepdims=True), extra)
    synthesis(rhs_ref, seeds_ref, x_ref, step_ref, norm_ref, side_ref, spec_ref, extra, out_ref)


def second_kernel(
    mine_ref, theirs_ref, rhs_ref, told_ref, keep_ref, other_ref, x_ref, step_ref, norm_ref, side_ref,
    out_ref, res_ref, alpha_ref, spec_ref, seeds_ref,
):
    load_seeds(keep_ref, other_ref, seeds_ref)
    prior = load_prior(keep_ref, other_ref)
    told = told_ref[...]
    norm_now = lane_total(told, 0) * 0.125
    energy = lane_total(told, 1) * 0.125
    pixels = lane_total(mine_ref[2 * NBP] + theirs_ref[2 * NBP], 64)
    alpha = norm_now / (energy + pixels)
    alpha_ref[...] = jnp.broadcast_to(alpha, (8, 128))
    residual = []
    for row in range(2 * NBP):
        image = prior[row] * rhs_ref[row] + (mine_ref[row] + theirs_ref[swapped(row)])
        residual.append(rhs_ref[row] - alpha * image)
        res_ref[row] = residual[row]
    squares = sum_rows([value * value for value in residual])
    extra = jnp.where(lanes() == 64, jnp.sum(squares, axis=1, keepdims=True), 0.0)
    synthesis(res_ref, seeds_ref, x_ref, step_ref, norm_ref, side_ref, spec_ref, extra, out_ref)


def last_kernel(
    mine_ref, theirs_ref, keep_ref, rhs_ref, res_ref, dir_ref, told_ref, alpha_ref, sol_ref, out_ref
):
    norm_now = lane_total(told_ref[...], 0) * 0.125
    energy = lane_total(mine_ref[2 * NBP], 65)
    pixels = lane_total(mine_ref[2 * NBP] + theirs_ref[2 * NBP], 64)
    alpha = norm_now / (energy + pixels)
    for block in range(2):
        for part in range(2):
            row = 2 * block + part
            image = keep_ref[block, part, :, LOOPS:] * dir_ref[row] + (mine_ref[row] + theirs_ref[swapped(row)])
            sol_ref[:, block, part, :] = alpha_ref[...] * rhs_ref[row] + alpha * dir_ref[row]
            out_ref[:, block, part, :] = res_ref[row] - alpha * image


def first_step(*arrays):
    return call(first_kernel, (PAYLOAD, COEF), LEGENDRE, "first", arrays)


def second_step(*arrays):
    return call(second_kernel, (PAYLOAD, COEF, TILE), LEGENDRE, "second", arrays)


def last_step(*arrays):
    result = jax.ShapeDtypeStruct((8, 2, 2, 128), F32)
    return call(last_kernel, (result, result), [], "last", arrays)


CHUNK = 256


def dot3(left, right_ref, spot):
    high, low = left
    rows = high.shape[0]
    both = jnp.dot(jnp.concatenate([high, low], axis=0), right_ref[0, :, spot], preferred_element_type=F32)
    return both[:rows] + both[rows:] + jnp.dot(high, right_ref[1, :, spot], preferred_element_type=F32)


def dot3_turned(left, right_ref, spot):
    high, low = left
    dims = (((1,), (1,)), ((), ()))
    rows = high.shape[0]
    both = lax.dot_general(jnp.concatenate([high, low], axis=0), right_ref[0, spot, :], dims, preferred_element_type=F32)
    return both[:rows] + both[rows:] + lax.dot_general(high, right_ref[1, spot, :], dims, preferred_element_type=F32)


def column_sums(even, odd, first, cos_ref, sin_ref, phase_ref):
    parts = [[], []]
    count = even[0].shape[0] // RH
    for at in range(0, NCOL, CHUNK):
        spot = slice(at, at + CHUNK)
        along = dot3(even, cos_ref, spot).reshape(count, RH, CHUNK)
        across = dot3(odd, sin_ref, spot).reshape(count, RH, CHUNK)
        real = jnp.zeros((RH, CHUNK), F32)
        imag = jnp.zeros((RH, CHUNK), F32)
        for section in range(count):
            row = first + section
            cos = phase_ref[0, row : row + 1, spot]
            sin = phase_ref[1, row : row + 1, spot]
            real = real + (cos * along[section] - sin * across[section])
            imag = imag - (cos * across[section] + sin * along[section])
        parts[0].append(real)
        parts[1].append(imag)
    return [jnp.concatenate(part, axis=1) for part in parts]


def pack(parts, extra, out_ref):
    rows = []
    for whole in parts:
        rows += [whole[:, :NPAIRS], whole[:, NPAIRS:]]
    whole = jnp.concatenate(rows + [extra, jnp.zeros((56, NPAIRS), F32)], axis=0)
    for at in range(0, NPAIRS, 128):
        turned = jnp.transpose(whole[:, at : at + 128])
        out_ref[at // 8 : at // 8 + 16] = turned.reshape(16, 8, 128)


def circle(cycles):
    quarter = lax.shift_right_logical(cycles + PERIOD // 8, 14)
    angle = (cycles - quarter * (PERIOD // 4)).astype(F32) * (2.0 * math.pi / PERIOD)
    square = angle * angle
    sin = angle * (1.0 + square * (-1 / 6 + square * (1 / 120 + square * (-1 / 5040 + square * (1 / 362880)))))
    cos = 1.0 + square * (-0.5 + square * (1 / 24 + square * (-1 / 720 + square * (1 / 40320))))
    odd = (quarter & 1) == 1
    cos, sin = jnp.where(odd, sin, cos), jnp.where(odd, cos, sin)
    cos = jnp.where((quarter == 1) | (quarter == 2), -cos, cos)
    sin = jnp.where((quarter == 2) | (quarter == 3), -sin, sin)
    return cos, sin


PIECES = 1
ANY = pl.BlockSpec(memory_space=pl.ANY)


def table_kernel(
    place_ref, noise_hbm, sky_hbm, m_ref, away_ref, heavy_ref, mine_ref, cos_ref, sin_ref, phase_ref, sky_ref, noise_ref, sems
):
    rep = place_ref[1]
    width = NPHI // 2 // PIECES
    copies = []
    for half, (row, noise) in enumerate(((1 - rep, away_ref), (rep, noise_ref))):
        rows = pl.ds(pl.multiple_of(RH * row, RH), RH)
        for piece in range(PIECES):
            spot = pl.ds(piece * width, width)
            for which, (source, target) in enumerate(((noise_hbm, noise), (sky_hbm, sky_ref.at[half]))):
                sem = sems.at[half, which, piece]
                copies.append(pltpu.make_async_copy(source.at[rows, spot], target.at[:, spot], sem))
                copies[-1].start()
    every_m = jnp.concatenate([m_ref[0:1, :], m_ref[1:2, :]], axis=1)

    def angles(rows, factor):
        return circle((factor(lax.broadcasted_iota(jnp.int32, (rows, NCOL), 0)) * every_m) & (PERIOD - 1))

    c_coarse, s_coarse = angles(COARSE, lambda row: 2 * FINE * row)
    c_fine, s_fine = angles(FINE, lambda row: 2 * row + 1)
    for row in range(COARSE):
        c_one, s_one = c_coarse[row : row + 1], s_coarse[row : row + 1]
        spot = slice(FINE * row, FINE * row + FINE)
        high, low = split(c_one * c_fine - s_one * s_fine)
        cos_ref[0, spot, :] = high
        cos_ref[1, spot, :] = low
        high, low = split(s_one * c_fine + c_one * s_fine)
        sin_ref[0, spot, :] = high
        sin_ref[1, spot, :] = low

    def centre(row):
        section = (row + OUTER // 2 * rep) & (OUTER - 1)
        return 2 * SECTION * section + SECTION - 1

    cos, sin = angles(OUTER, centre)
    phase_ref[0] = cos
    phase_ref[1] = sin
    for half, (noise, out) in enumerate(((away_ref, heavy_ref), (noise_ref, mine_ref))):
        for piece in range(PIECES):
            at = 2 * (half * PIECES + piece)
            copies[at].wait()
            copies[at + 1].wait()
            spot = slice(piece * width, (piece + 1) * width)
            out[:, spot] = noise[:, spot] * sky_ref[half, :, spot]


def tables(place, noise, sky, every_m):
    pixels = pltpu.VMEM((RH, NPHI // 2), F32)
    return pl.pallas_call(
        table_kernel,
        in_specs=[SMEM, ANY, ANY, VMEM],
        out_specs=(VMEM,) * 6,
        out_shape=(pixels, pixels, pixels, TABLE, TABLE, PHASES),
        scratch_shapes=[pltpu.VMEM((2, RH, NPHI // 2), F32), pixels, pltpu.SemaphoreType.DMA((2, 2, PIECES))],
        compiler_params=pltpu.CompilerParams(vmem_limit_bytes=LIMIT),
        name="tables",
    )(place, *far(noise, sky), *held(every_m))


def folded(ref, offset):
    count = OUTER // 2
    return jnp.concatenate([ref[:, SECTION * b + offset : SECTION * b + offset + HALF] for b in range(count)], axis=0)


def turned(rows):
    down = lax.broadcasted_iota(jnp.int32, (256, 256), 0)
    along = lax.broadcasted_iota(jnp.int32, (256, 256), 1)
    flip = jnp.where(down + along == 255, 1.0, 0.0).astype(BF16)
    pieces = []
    for at in (256, 0):
        high, low = split(rows[:, at : at + 256])
        pieces.append(jnp.dot(high, flip, preferred_element_type=F32) + jnp.dot(low, flip, preferred_element_type=F32))
    return jnp.concatenate(pieces, axis=1)


def half_sums(ref, first, cos_ref, sin_ref, phase_ref):
    ahead = folded(ref, HALF) * SCALE
    back = turned(folded(ref, 0)) * SCALE
    return column_sums(split(ahead + back), split(ahead - back), first, cos_ref, sin_ref, phase_ref)


def own_kernel(mine_ref, cos_ref, sin_ref, phase_ref, sums_ref):
    sums_ref[0], sums_ref[1] = half_sums(mine_ref, 0, cos_ref, sin_ref, phase_ref)


def sky_kernel(heavy_ref, sums_ref, cos_ref, sin_ref, phase_ref, out_ref):
    parts = half_sums(heavy_ref, OUTER // 2, cos_ref, sin_ref, phase_ref)
    pack([sums_ref[0] + parts[0], sums_ref[1] + parts[1]], jnp.zeros((8, NPAIRS), F32), out_ref)


def own_step(*arrays):
    return call(own_kernel, pltpu.VMEM((2, RH, NCOL), F32), [], "own", arrays)


def sky_step(*arrays):
    return call(sky_kernel, PAYLOAD, [], "sky", arrays)


def noise_kernel(rep_ref, noise_ref, other_ref, plus_ref, minus_ref):
    for half, ref in enumerate((noise_ref, other_ref)):
        spot = slice(half * ROWS // 2, (half + 1) * ROWS // 2)
        plus_ref[spot, :] = folded(ref, HALF) * (SCALE * SCALE)
        minus_ref[spot, :] = turned(folded(ref, 0)) * (SCALE * SCALE)


OWN = pl.BlockSpec((RH, NPHI // 2), lambda i, rep: (rep[0], 0))


def noise_step(rep, noise, other):
    return pl.pallas_call(
        noise_kernel,
        grid_spec=pltpu.PrefetchScalarGridSpec(
            num_scalar_prefetch=1, grid=(1,), in_specs=[OWN, VMEM], out_specs=(VMEM, VMEM)
        ),
        out_shape=(PIXELS, PIXELS),
        compiler_params=pltpu.CompilerParams(vmem_limit_bytes=LIMIT),
        name="noise",
    )(rep, *far(noise), *held(other))


def by_rows(recv_ref):
    flat = recv_ref[...].reshape(NPAIRS, 128)
    return jnp.concatenate([jnp.transpose(flat[at : at + 128]) for at in range(0, NPAIRS, 128)], axis=1)


def fetch(places, holders, sems):
    copies = [pltpu.make_async_copy(a, b, sems.at[i]) for i, (a, b) in enumerate(zip(places, holders))]
    for copy in copies:
        copy.start()
    return copies


def through_map(rows, energy, copies, holders, phase_ref, out_ref, mixed_ref, even_ref, odd_ref):
    cos_ref, sin_ref, plus_ref, minus_ref = holders
    real = jnp.concatenate([rows[0:RH], rows[RH : 2 * RH]], axis=1)
    imag = jnp.concatenate([rows[2 * RH : 3 * RH], rows[3 * RH : 4 * RH]], axis=1)
    for section in range(OUTER):
        cos = phase_ref[0, section : section + 1, :]
        sin = phase_ref[1, section : section + 1, :]
        spot = slice(section * RH, section * RH + RH)
        high, low = split(real * cos - imag * sin)
        mixed_ref[0, spot, :] = high
        mixed_ref[1, spot, :] = low
        high, low = split(real * sin + imag * cos)
        mixed_ref[2, spot, :] = high
        mixed_ref[3, spot, :] = low
    spots = [slice(at, at + CHUNK) for at in range(0, HALF, CHUNK)]
    evens = [dot3_turned((mixed_ref[0], mixed_ref[1]), cos_ref, spot) for spot in spots]
    copies[0].wait()
    odds = [dot3_turned((mixed_ref[2], mixed_ref[3]), sin_ref, spot) for spot in spots]
    copies[1].wait()
    copies[2].wait()
    power = jnp.zeros((ROWS, 128), F32)
    for spot, even, odd in zip(spots, evens, odds):
        ahead = even - odd
        back = even + odd
        heavy_ahead = plus_ref[:, spot] * ahead
        heavy_back = minus_ref[:, spot] * back
        terms = heavy_ahead * ahead + heavy_back * back
        for piece in range(0, CHUNK, 128):
            power = power + terms[:, piece : piece + 128]
        high, low = split(heavy_ahead + heavy_back)
        even_ref[0, :, spot] = high
        even_ref[1, :, spot] = low
        high, low = split(heavy_ahead - heavy_back)
        odd_ref[0, :, spot] = high
        odd_ref[1, :, spot] = low
    pixels = total_of(power)
    lane = lanes(8, NPAIRS)
    row = lax.broadcasted_iota(jnp.int32, (8, NPAIRS), 0)
    extra = jnp.where((lane % 8 == 0) & (row == 0), pixels, 0.0)
    extra = jnp.where((lane % 8 == 0) & (row == 1), energy, extra)
    parts = column_sums((even_ref[0], even_ref[1]), (odd_ref[0], odd_ref[1]), 0, cos_ref, sin_ref, phase_ref)
    pack(parts, extra, out_ref)


def row_total(rows, index):
    return jnp.sum(rows[index : index + 1], axis=1, keepdims=True)


def map_one_kernel(
    recv_ref, phase_ref, cos_ref, sin_hbm, plus_hbm, minus_hbm,
    out_ref, told_ref, mixed_ref, even_ref, odd_ref, sin_ref, plus_ref, minus_ref, sems,
):
    holders = (cos_ref, sin_ref, plus_ref, minus_ref)
    copies = fetch((sin_hbm, plus_hbm, minus_hbm), holders[1:], sems)
    rows = by_rows(recv_ref)
    lane = lanes()
    told = jnp.where(lane == 0, row_total(rows, 64), 0.0)
    told_ref[...] = jnp.where(lane == 1, row_total(rows, 65), told)
    through_map(rows, jnp.zeros((1, 1), F32), copies, holders, phase_ref, out_ref, mixed_ref, even_ref, odd_ref)


def map_two_kernel(
    recv_ref, before_ref, told_ref, keep_ref, other_ref, rhs_ref, res_ref, phase_ref, cos_ref, sin_hbm, plus_hbm, minus_hbm,
    out_ref, dir_ref, told_out_ref, mixed_ref, even_ref, odd_ref, sin_ref, plus_ref, minus_ref, sems,
):
    holders = (cos_ref, sin_ref, plus_ref, minus_ref)
    copies = fetch((sin_hbm, plus_hbm, minus_hbm), holders[1:], sems)
    rows = by_rows(recv_ref)
    norm_next = row_total(rows, 64)
    beta = norm_next / (lane_total(told_ref[...], 0) * 0.125)
    told_out_ref[...] = jnp.where(lanes() == 0, norm_next, 0.0)
    prior = load_prior(keep_ref, other_ref)
    terms = []
    for row in range(2 * NBP):
        value = res_ref[row] + beta * rhs_ref[row]
        dir_ref[row] = value
        terms.append(prior[row] * value * value)
    energy = sum_rows(terms)
    rows = rows + beta * by_rows(before_ref)
    through_map(rows, total_of(energy), copies, holders, phase_ref, out_ref, mixed_ref, even_ref, odd_ref)


def map_call(kernel, outs, name, arrays, tables_and_noise):
    half = pltpu.VMEM((2, ROWS, HALF), BF16)
    return pl.pallas_call(
        kernel,
        in_specs=[VMEM] * len(arrays) + [ANY] * 3,
        out_specs=jax.tree.map(lambda _: VMEM, outs),
        out_shape=outs,
        scratch_shapes=[
            pltpu.VMEM((4, ROWS, NCOL), BF16), half, half,
            pltpu.VMEM((2, HALF, NCOL), BF16),
            pltpu.VMEM((ROWS, HALF), F32), pltpu.VMEM((ROWS, HALF), F32),
            pltpu.SemaphoreType.DMA((3,)),
        ],
        compiler_params=pltpu.CompilerParams(vmem_limit_bytes=LIMIT),
        name=name,
    )(*held(*arrays), *far(*tables_and_noise))


def map_one(*arrays):
    return map_call(map_one_kernel, (PAYLOAD, TILE), "map_one", arrays[:-3], arrays[-3:])


def map_two(*arrays):
    return map_call(map_two_kernel, (PAYLOAD, COEF, TILE), "map_two", arrays[:-3], arrays[-3:])


def shards(sky_map, noise_weight, prior_weight, seeds, loop_cos, pair_m, block_count):
    rep = lax.axis_index("rep")
    rep_array = jnp.reshape(rep, (1,)).astype(jnp.int32)
    place = jnp.stack([lax.axis_index("blk"), rep]).astype(jnp.int32)

    def swap(value):
        return lax.ppermute(value, "rep", [(0, 1), (1, 0)])

    def transpose(payload):
        return lax.all_to_all(payload, "blk", split_axis=0, concat_axis=0, tiled=True)

    every_m = jnp.transpose(pair_m)
    noise_away, heavy, mine, cos, sin, phases = tables(place, noise_weight, sky_map, every_m)
    heavy = swap(heavy)
    sums = own_step(mine, cos, sin, phases)
    payload = sky_step(heavy, sums, cos, sin, phases)
    recv = transpose(payload)

    payload, place, noise_away = lax.optimization_barrier((payload, place, noise_away))
    plus, minus = noise_step(rep_array, noise_weight, swap(noise_away))
    keep, send, x, step, norm, side = prepare(place, block_count, seeds, prior_weight, loop_cos[None, :], every_m)
    other = swap(send)
    legendre = (keep, other, x, step, norm, side)

    recv, plus, minus = lax.optimization_barrier((recv, plus, minus))
    here = analysis(recv, *legendre)
    payload, rhs = first_step(here, swap(here), *legendre)
    before = transpose(payload)
    payload, told = map_one(before, phases, cos, sin, plus, minus)
    here = analysis(transpose(payload), *legendre)
    payload, residual, alpha = second_step(here, swap(here), rhs, told, *legendre)
    payload, direction, told = map_two(
        transpose(payload), before, told, keep, other, rhs, residual, phases, cos, sin, plus, minus
    )
    here = analysis(transpose(payload), *legendre)
    return last_step(here, swap(here), keep, rhs, residual, direction, told, alpha)


def solution(mesh):
    placed = (
        P("blk", "rep"),
        P("blk", "rep"),
        P("blk", "rep", None, None),
        P("blk", "rep", None, None),
        P(),
        P(),
        P("blk"),
    )
    return jax.shard_map(
        shards,
        mesh=mesh,
        in_specs=placed,
        out_specs=(P("blk", "rep", None, None), P("blk", "rep", None, None)),
        check_vma=False,
    )
```
